32 devices in a mesh: wide: 16 (over z, y, x), chain: 2 (over core).
Axes of the slice: x: 2, y: 2, z: 4, core: 2. Of those that a mesh axis runs over, the one named last changes fastest.
Arguments:
- queries: bfloat16 [8192, 1024], P(('chain', 'wide')), may hold values from -4 to 4
- keys: bfloat16 [8192, 1024], P(('chain', 'wide')), may hold values from -4 to 4
- values: bfloat16 [8192, 1024], P(('chain', 'wide')), may hold values from -6 to 6
Outputs:
- attended: bfloat16 [8192, 1024], P(('chain', 'wide'))
The draws below stay inside these ranges and needn't reach their ends.
All inputs are finite; a program needn't handle non-finite values.
Results may differ from the reference program's by a relative error of at most 0.005.
Values may be sent and summed in bfloat16 or wider, within the bound.
No kernel may reach another device: no remote copies, remote signals or barrier semaphores. Data moves between devices by JAX's collectives and lax.ppermute only.
A program may use at most 64 MiB of HBM per device.

```python
import jax
import jax.numpy as jnp
from jax import lax

HEADS = 16
HEAD_DIM = 64
TOK_DEV = 256
TOKENS = 8192


def level_of(rng, shape, cuts, least, high):
    def one(position, parts):
        steps = jax.random.uniform(jax.random.fold_in(jax.random.fold_in(rng, 6), position), (parts,), jnp.float32, least / len(cuts), high / len(cuts))
        return jnp.repeat(jnp.exp(steps), shape[position] // parts).reshape((-1,) + (1,) * (len(shape) - position - 1))

    gain = one(*cuts[0])
    for cut in cuts[1:]:
        gain = gain * one(*cut)
    return gain


def scatter_about(rng, extent, width, limit, pieces=(), dtype=jnp.bfloat16):
    level = level_of(rng, extent, pieces, -0.22, 0.18) if pieces else 1.0
    drawn = jax.random.normal(rng, extent, jnp.float32) * width * level
    return jnp.minimum(jnp.maximum(drawn, -limit), limit).astype(dtype)


def setup_inputs(seed: int = 0) -> dict:
    splits = jax.random.split(jax.random.key(seed), 4)
    queries = scatter_about(splits[0], (TOKENS, HEADS * HEAD_DIM), 0.3, 4.0, ((0, 32),))
    keys = scatter_about(splits[1], (TOKENS, HEADS * HEAD_DIM), 0.3, 4.0, ((0, 32),))
    values = scatter_about(splits[2], (TOKENS, HEADS * HEAD_DIM), 1.0, 6.0, ((0, 32),))
    return {"queries": queries, "keys": keys, "values": values}


def reference(queries, keys, values):
    blocks = TOKENS // TOK_DEV
    q_all = queries.reshape(blocks, TOK_DEV, HEADS, HEAD_DIM)
    k_all = keys.reshape(blocks, TOK_DEV, HEADS, HEAD_DIM)
    v_all = values.reshape(blocks, TOK_DEV, HEADS, HEAD_DIM)
    causal = jnp.arange(TOK_DEV)[:, None] >= jnp.arange(TOK_DEV)[None, :]

    def advance(carry, block):
        q_blk, k_blk, v_blk = block
        q32 = q_blk.astype(jnp.float32)
        k32 = k_blk.astype(jnp.float32)
        v32 = v_blk.astype(jnp.float32)
        prefix = carry.astype(jnp.bfloat16).astype(jnp.float32)
        inter = jnp.einsum('the,hef->thf', q32, prefix)
        scores = jnp.einsum('the,she->hts', q32, k32)
        scores = jnp.where(causal[None], scores, 0.0).astype(jnp.bfloat16).astype(jnp.float32)
        intra = jnp.einsum('hts,shf->thf', scores, v32)
        total = intra + inter
        normed = total / jnp.sqrt(lax.optimization_barrier(jnp.mean(total * total, axis=-1, keepdims=True)) + 1e-06)
        state = jnp.einsum('the,thf->hef', k32, v32)
        return (carry + state, normed.astype(jnp.bfloat16))
    start = jnp.zeros((HEADS, HEAD_DIM, HEAD_DIM), jnp.float32)
    final_state, outputs = lax.scan(advance, start, (q_all, k_all, v_all))
    return outputs.reshape(TOKENS, HEADS * HEAD_DIM)
```

```python
import functools

import jax
import jax.numpy as jnp
from jax import lax
from jax.experimental import pallas as pl
from jax.experimental.pallas import tpu as pltpu
from jax.sharding import PartitionSpec as P

HEADS = 16
HEAD_DIM = 64
PAIRS = HEADS // 2
LANES = 2 * HEAD_DIM
AXES = ("chain", "wide")
VMEM = pl.BlockSpec(memory_space=pltpu.VMEM)


def first_head(shape):
    return lax.broadcasted_iota(jnp.int32, shape, len(shape) - 1) < HEAD_DIM


def lanes_of(p):
    return slice(p * LANES, (p + 1) * LANES)


def rows_of(p):
    return slice(p * HEAD_DIM, (p + 1) * HEAD_DIM)


def states_kernel(k_ref, v_ref, out_ref):
    first = first_head((HEAD_DIM, LANES))
    for p in range(PAIRS):
        both = lax.dot_general(
            k_ref[:, lanes_of(p)], v_ref[:, lanes_of(p)], (((0,), (0,)), ((), ())),
            preferred_element_type=jnp.float32)
        packed = jnp.where(first, both[:HEAD_DIM], both[HEAD_DIM:])
        out_ref[rows_of(p), :] = packed.astype(out_ref.dtype)


def scan_kernel(x_ref, out_ref):
    parts = x_ref.shape[0]
    total = jnp.zeros(x_ref.shape[1:], jnp.float32)
    for i in range(parts):
        out_ref[i] = total.astype(out_ref.dtype)
        if i < parts - 1:
            total = total + x_ref[i].astype(jnp.float32)


def scan_rows_kernel(x_ref, out_ref):
    parts = x_ref.shape[0]
    row = lax.broadcasted_iota(jnp.int32, (parts, parts), 0)
    col = lax.broadcasted_iota(jnp.int32, (parts, parts), 1)
    below = jnp.where(col < row, 1.0, 0.0).astype(jnp.bfloat16)
    out_ref[...] = jnp.dot(below, x_ref[...], preferred_element_type=jnp.float32).astype(out_ref.dtype)


def attend_kernel(q_ref, k_ref, v_ref, prefix_ref, out_ref):
    rows = q_ref.shape[0]
    causal = (lax.broadcasted_iota(jnp.int32, (rows, rows), 0)
              >= lax.broadcasted_iota(jnp.int32, (rows, rows), 1))
    first = first_head((rows, LANES))
    first_state = first_head((HEAD_DIM, LANES))
    same = (first_head((LANES, LANES))
            == (lax.broadcasted_iota(jnp.int32, (LANES, LANES), 0) < HEAD_DIM))
    ones = jnp.where(same, 1.0, 0.0).astype(jnp.bfloat16)
    zero = jnp.zeros((), jnp.bfloat16)
    for p in range(PAIRS):
        q, k, v = q_ref[:, lanes_of(p)], k_ref[:, lanes_of(p)], v_ref[:, lanes_of(p)]
        intra = []
        for mine in (first, ~first):
            scores = lax.dot_general(
                jnp.where(mine, q, zero), k, (((1,), (1,)), ((), ())),
                preferred_element_type=jnp.float32)
            scores = jnp.where(causal, scores, 0.0).astype(jnp.bfloat16)
            intra.append(jnp.dot(scores, v, preferred_element_type=jnp.float32))
        packed = prefix_ref[rows_of(p), :]
        prefix = jnp.concatenate(
            [jnp.where(first_state, packed, zero), jnp.where(first_state, zero, packed)], axis=0)
        inter = jnp.dot(q, prefix, preferred_element_type=jnp.float32)
        total = jnp.where(first, intra[0], intra[1]) + inter
        square = total * total
        high = square.astype(jnp.bfloat16)
        low = (square - high.astype(jnp.float32)).astype(jnp.bfloat16)
        sums = (jnp.dot(high, ones, preferred_element_type=jnp.float32)
                + jnp.dot(low, ones, preferred_element_type=jnp.float32))
        out_ref[:, lanes_of(p)] = (total * lax.rsqrt(sums * (1.0 / HEAD_DIM) + 1e-6)).astype(out_ref.dtype)


def call(kernel, shape, dtype, *args, flops=0):
    moved = sum(a.size * a.dtype.itemsize for a in args)
    return pl.pallas_call(
        kernel,
        out_shape=jax.ShapeDtypeStruct(shape, dtype),
        in_specs=[VMEM] * len(args),
        out_specs=VMEM,
        cost_estimate=pl.CostEstimate(flops=flops, bytes_accessed=moved, transcendentals=0),
        compiler_params=pltpu.CompilerParams(vmem_limit_bytes=32 * 1024 * 1024),
    )(*args)


def per_device(parts, queries, keys, values):
    rows = queries.shape[0]
    state_rows = PAIRS * HEAD_DIM
    share = state_rows // parts
    states = call(states_kernel, (state_rows, LANES), jnp.bfloat16, keys, values,
                  flops=2 * rows * LANES * LANES * PAIRS)
    view = (parts, share, LANES) if share > 1 else (parts, LANES)
    mine = lax.all_to_all(states.reshape(view), AXES, 0, 0, tiled=True)
    before = call(scan_kernel if share > 1 else scan_rows_kernel, view, jnp.bfloat16, mine)
    prefix = lax.all_to_all(before, AXES, 0, 0, tiled=True).reshape(state_rows, LANES)
    return call(attend_kernel, queries.shape, jnp.bfloat16, queries, keys, values, prefix,
                flops=4 * rows * rows * HEADS * HEAD_DIM)


def solution(mesh):
    spec = P(AXES, None)
    parts = mesh.shape["chain"] * mesh.shape["wide"]
    return jax.shard_map(
        functools.partial(per_device, parts),
        mesh=mesh,
        in_specs=(spec, spec, spec),
        out_specs=spec,
        check_vma=False,
    )
```

```python
import functools

import jax
import jax.numpy as jnp
from jax import lax
from jax.experimental import pallas as pl
from jax.experimental.pallas import tpu as pltpu
from jax.sharding import PartitionSpec as P

HEADS = 16
HEAD_DIM = 64
PAIRS = HEADS // 2
LANES = 2 * HEAD_DIM
SLABS = 4
SLAB = HEADS * HEAD_DIM // SLABS
AXES = ("chain", "wide")
HBM = pl.BlockSpec(memory_space=pltpu.HBM)
VMEM = pl.BlockSpec(memory_space=pltpu.VMEM)


def first_head(shape):
    return lax.broadcasted_iota(jnp.int32, shape, len(shape) - 1) < HEAD_DIM


def lanes_of(p):
    return slice(p * LANES, (p + 1) * LANES)


def rows_of(p):
    return slice(p * HEAD_DIM, (p + 1) * HEAD_DIM)


def states_kernel(k_hbm, v_hbm, out_ref, k_ref, v_ref, arrived):
    copies = []
    for s in range(SLABS):
        lanes = slice(s * SLAB, (s + 1) * SLAB)
        copies.append([
            pltpu.make_async_copy(k_hbm.at[:, lanes], k_ref.at[:, lanes], arrived.at[0, s]),
            pltpu.make_async_copy(v_hbm.at[:, lanes], v_ref.at[:, lanes], arrived.at[1, s])])
        for copy in copies[-1]:
            copy.start()
    first = first_head((HEAD_DIM, LANES))
    for p in range(PAIRS):
        if p * LANES % SLAB == 0:
            for copy in copies[p * LANES // SLAB]:
                copy.wait()
        both = lax.dot_general(
            k_ref[:, lanes_of(p)], v_ref[:, lanes_of(p)], (((0,), (0,)), ((), ())),
            preferred_element_type=jnp.float32)
        packed = jnp.where(first, both[:HEAD_DIM], both[HEAD_DIM:])
        out_ref[rows_of(p), :] = packed.astype(out_ref.dtype)


def scan_kernel(x_ref, out_ref):
    parts = x_ref.shape[0]
    total = jnp.zeros(x_ref.shape[1:], jnp.float32)
    for i in range(parts):
        out_ref[i] = total.astype(out_ref.dtype)
        if i < parts - 1:
            total = total + x_ref[i].astype(jnp.float32)


def scan_rows_kernel(x_ref, out_ref):
    parts = x_ref.shape[0]
    row = lax.broadcasted_iota(jnp.int32, (parts, parts), 0)
    col = lax.broadcasted_iota(jnp.int32, (parts, parts), 1)
    below = jnp.where(col < row, 1.0, 0.0).astype(jnp.bfloat16)
    out_ref[...] = jnp.dot(below, x_ref[...], preferred_element_type=jnp.float32).astype(out_ref.dtype)


def intra_kernel(q_ref, k_ref, v_ref, out_ref):
    rows = q_ref.shape[0]
    causal = (lax.broadcasted_iota(jnp.int32, (rows, rows), 0)
              >= lax.broadcasted_iota(jnp.int32, (rows, rows), 1))
    first = first_head((rows, LANES))
    zero = jnp.zeros((), jnp.bfloat16)
    for p in range(PAIRS):
        q, k, v = q_ref[:, lanes_of(p)], k_ref[:, lanes_of(p)], v_ref[:, lanes_of(p)]
        intra = []
        for mine in (first, ~first):
            scores = lax.dot_general(
                jnp.where(mine, q, zero), k, (((1,), (1,)), ((), ())),
                preferred_element_type=jnp.float32)
            scores = jnp.where(causal, scores, 0.0).astype(jnp.bfloat16)
            intra.append(jnp.dot(scores, v, preferred_element_type=jnp.float32))
        out_ref[:, lanes_of(p)] = jnp.where(first, intra[0], intra[1])


def attend_kernel(q_ref, intra_ref, prefix_ref, out_ref):
    first_state = first_head((HEAD_DIM, LANES))
    same = (first_head((LANES, LANES))
            == (lax.broadcasted_iota(jnp.int32, (LANES, LANES), 0) < HEAD_DIM))
    ones = jnp.where(same, 1.0, 0.0).astype(jnp.bfloat16)
    zero = jnp.zeros((), jnp.bfloat16)
    for p in range(PAIRS):
        packed = prefix_ref[rows_of(p), :]
        prefix = jnp.concatenate(
            [jnp.where(first_state, packed, zero), jnp.where(first_state, zero, packed)], axis=0)
        inter = jnp.dot(q_ref[:, lanes_of(p)], prefix, preferred_element_type=jnp.float32)
        total = intra_ref[:, lanes_of(p)] + inter
        square = total * total
        high = square.astype(jnp.bfloat16)
        low = (square - high.astype(jnp.float32)).astype(jnp.bfloat16)
        sums = (jnp.dot(high, ones, preferred_element_type=jnp.float32)
                + jnp.dot(low, ones, preferred_element_type=jnp.float32))
        out_ref[:, lanes_of(p)] = (total * lax.rsqrt(sums * (1.0 / HEAD_DIM) + 1e-6)).astype(out_ref.dtype)


def call(kernel, shape, dtype, *args, flops=0, memory=VMEM, scratch=(), limit=16):
    moved = sum(a.size * a.dtype.itemsize for a in args)
    return pl.pallas_call(
        kernel,
        out_shape=jax.ShapeDtypeStruct(shape, dtype),
        in_specs=[memory] * len(args),
        out_specs=VMEM,
        scratch_shapes=scratch,
        cost_estimate=pl.CostEstimate(flops=flops, bytes_accessed=moved, transcendentals=0),
        compiler_params=pltpu.CompilerParams(vmem_limit_bytes=limit * 1024 * 1024),
    )(*args)


def per_device(parts, queries, keys, values):
    rows = queries.shape[0]
    state_rows = PAIRS * HEAD_DIM
    share = state_rows // parts
    states = call(states_kernel, (state_rows, LANES), jnp.bfloat16, keys, values,
                  flops=2 * rows * LANES * LANES * PAIRS, memory=HBM, limit=60,
                  scratch=[pltpu.VMEM(keys.shape, keys.dtype), pltpu.VMEM(values.shape, values.dtype),
                           pltpu.SemaphoreType.DMA((2, SLABS))])
    intra = call(intra_kernel, queries.shape, jnp.float32, queries, keys, values,
                 flops=4 * rows * rows * HEADS * HEAD_DIM)
    view = (parts, share, LANES) if share > 1 else (parts, LANES)
    mine = lax.all_to_all(states.reshape(view), AXES, 0, 0, tiled=True)
    before = call(scan_kernel if share > 1 else scan_rows_kernel, view, jnp.bfloat16, mine)
    prefix = lax.all_to_all(before, AXES, 0, 0, tiled=True).reshape(state_rows, LANES)
    return call(attend_kernel, queries.shape, jnp.bfloat16, queries, intra, prefix,
                flops=2 * rows * HEAD_DIM * HEAD_DIM * HEADS)


def solution(mesh):
    spec = P(AXES, None)
    parts = mesh.shape["chain"] * mesh.shape["wide"]
    return jax.shard_map(
        functools.partial(per_device, parts),
        mesh=mesh,
        in_specs=(spec, spec, spec),
        out_specs=spec,
        check_vma=False,
    )
```

```python
import functools

import jax
import jax.numpy as jnp
from jax import lax
from jax.experimental import pallas as pl
from jax.experimental.pallas import tpu as pltpu
from jax.sharding import PartitionSpec as P

HEADS = 16
HEAD_DIM = 64
PAIRS = HEADS // 2
LANES = 2 * HEAD_DIM
SLABS = 4
SLAB = HEADS * HEAD_DIM // SLABS
VMEM = pl.BlockSpec(memory_space=pltpu.VMEM)


def first_head(shape):
    return lax.broadcasted_iota(jnp.int32, shape, len(shape) - 1) < HEAD_DIM


def lanes_of(p):
    return slice(p * LANES, (p + 1) * LANES)


def rows_of(p):
    return slice(p * HEAD_DIM, (p + 1) * HEAD_DIM)


def states_kernel(k_hbm, v_hbm, out_ref, k_ref, v_ref, arrived):
    copies = []
    for s in range(SLABS):
        lanes = slice(s * SLAB, (s + 1) * SLAB)
        copies.append([
            pltpu.make_async_copy(k_hbm.at[:, lanes], k_ref.at[:, lanes], arrived.at[0, s]),
            pltpu.make_async_copy(v_hbm.at[:, lanes], v_ref.at[:, lanes], arrived.at[1, s])])
        for copy in copies[-1]:
            copy.start()
    first = first_head((HEAD_DIM, LANES))
    for p in range(PAIRS):
        if p * LANES % SLAB == 0:
            for copy in copies[p * LANES // SLAB]:
                copy.wait()
        both = lax.dot_general(
            k_ref[:, lanes_of(p)], v_ref[:, lanes_of(p)], (((0,), (0,)), ((), ())),
            preferred_element_type=jnp.float32)
        packed = jnp.where(first, both[:HEAD_DIM], both[HEAD_DIM:])
        out_ref[rows_of(p), :] = packed.astype(out_ref.dtype)


def totals_kernel(x_ref, out_ref):
    planes, chains = out_ref.shape[:2]
    inner = x_ref.shape[0] // chains
    for c in range(chains):
        total = x_ref[c * inner]
        for i in range(1, inner):
            total = total + x_ref[c * inner + i]
        for z in range(planes):
            out_ref[z, c] = total.astype(out_ref.dtype)


def prefix_kernel(x_ref, all_ref, out_ref):
    planes, chains = all_ref.shape[:2]
    inner = x_ref.shape[0] // chains
    plane = lax.axis_index("outer")
    groups = jnp.zeros(all_ref.shape[2:], jnp.float32)
    for c in range(chains):
        total = groups
        for z in range(planes):
            there = all_ref[z, c].astype(jnp.float32)
            total = total + jnp.where(z < plane, there, 0.0)
            groups = groups + there
        for i in range(inner):
            out_ref[c * inner + i] = total.astype(out_ref.dtype)
            if i < inner - 1:
                total = total + x_ref[c * inner + i]


def intra_kernel(q_ref, k_ref, v_ref, out_ref):
    rows = q_ref.shape[0]
    causal = (lax.broadcasted_iota(jnp.int32, (rows, rows), 0)
              >= lax.broadcasted_iota(jnp.int32, (rows, rows), 1))
    first = first_head((rows, LANES))
    zero = jnp.zeros((), jnp.bfloat16)
    for p in range(PAIRS):
        q, k, v = q_ref[:, lanes_of(p)], k_ref[:, lanes_of(p)], v_ref[:, lanes_of(p)]
        intra = []
        for mine in (first, ~first):
            scores = lax.dot_general(
                jnp.where(mine, q, zero), k, (((1,), (1,)), ((), ())),
                preferred_element_type=jnp.float32)
            scores = jnp.where(causal, scores, 0.0).astype(jnp.bfloat16)
            intra.append(jnp.dot(scores, v, preferred_element_type=jnp.float32))
        out_ref[:, lanes_of(p)] = jnp.where(first, intra[0], intra[1])


def attend_kernel(q_ref, intra_ref, prefix_ref, out_ref):
    first_state = first_head((HEAD_DIM, LANES))
    same = (first_head((LANES, LANES))
            == (lax.broadcasted_iota(jnp.int32, (LANES, LANES), 0) < HEAD_DIM))
    ones = jnp.where(same, 1.0, 0.0).astype(jnp.bfloat16)
    zero = jnp.zeros((), jnp.bfloat16)
    for p in range(PAIRS):
        packed = prefix_ref[rows_of(p), :]
        prefix = jnp.concatenate(
            [jnp.where(first_state, packed, zero), jnp.where(first_state, zero, packed)], axis=0)
        inter = jnp.dot(q_ref[:, lanes_of(p)], prefix, preferred_element_type=jnp.float32)
        total = intra_ref[:, lanes_of(p)] + inter
        square = total * total
        high = square.astype(jnp.bfloat16)
        low = (square - high.astype(jnp.float32)).astype(jnp.bfloat16)
        sums = (jnp.dot(high, ones, preferred_element_type=jnp.float32)
                + jnp.dot(low, ones, preferred_element_type=jnp.float32))
        out_ref[:, lanes_of(p)] = (total * lax.rsqrt(sums * (1.0 / HEAD_DIM) + 1e-6)).astype(out_ref.dtype)


def call(kernel, outs, *args, flops=0, scratch=(), memory=pltpu.VMEM):
    moved = sum(a.size * a.dtype.itemsize for a in args)
    single = not isinstance(outs, list)
    outs = [pltpu.VMEM(shape, dtype) for shape, dtype in ([outs] if single else outs)]
    args = [pltpu.with_memory_space_constraint(a, memory) for a in args]
    got = pl.pallas_call(
        kernel,
        out_shape=outs,
        in_specs=[pl.BlockSpec(memory_space=memory)] * len(args),
        out_specs=[VMEM] * len(outs),
        scratch_shapes=scratch,
        cost_estimate=pl.CostEstimate(flops=flops, bytes_accessed=moved, transcendentals=0),
        compiler_params=pltpu.CompilerParams(vmem_limit_bytes=16 * 1024 * 1024),
    )(*args)
    return got[0] if single else got


def per_device(chains, planes, inner, queries, keys, values):
    rows = queries.shape[0]
    members = chains * inner
    share = PAIRS * HEAD_DIM // members
    states, keys, values = call(
        states_kernel,
        [((PAIRS * HEAD_DIM, LANES), jnp.float32), (keys.shape, keys.dtype), (values.shape, values.dtype)],
        keys, values, flops=2 * rows * LANES * LANES * PAIRS, memory=pltpu.HBM,
        scratch=[pltpu.SemaphoreType.DMA((2, SLABS))])
    mine = lax.all_to_all(states.reshape(members, share, LANES), ("chain", "inner"), 0, 0, tiled=True)
    totals = call(totals_kernel, ((planes, chains, share, LANES), jnp.bfloat16), mine)
    totals = lax.all_to_all(totals, "outer", 0, 0, tiled=True)
    before = call(prefix_kernel, ((members, share, LANES), jnp.bfloat16), mine, totals)
    prefix = lax.all_to_all(before, ("chain", "inner"), 0, 0, tiled=True)
    intra = call(intra_kernel, (queries.shape, jnp.float32), queries, keys, values,
                 flops=4 * rows * rows * HEADS * HEAD_DIM)
    out = pl.pallas_call(
        attend_kernel,
        out_shape=jax.ShapeDtypeStruct(queries.shape, jnp.bfloat16),
        in_specs=[VMEM] * 3,
        out_specs=VMEM,
        compiler_params=pltpu.CompilerParams(vmem_limit_bytes=16 * 1024 * 1024),
    )(queries, intra, prefix.reshape(PAIRS * HEAD_DIM, LANES))
    return out


def solution(mesh):
    wide, chains = mesh.devices.shape
    inner = 4
    planes = wide // inner
    finer = jax.sharding.Mesh(mesh.devices.reshape(planes, inner, chains), ("outer", "inner", "chain"))
    spec = P(("chain", "outer", "inner"), None)
    return jax.shard_map(
        functools.partial(per_device, chains, planes, inner),
        mesh=finer,
        in_specs=(spec, spec, spec),
        out_specs=spec,
        check_vma=False,
    )
```

```python
import functools

import jax
import jax.numpy as jnp
from jax import lax
from jax.experimental import pallas as pl
from jax.experimental.pallas import tpu as pltpu
from jax.sharding import PartitionSpec as P

HEADS = 16
HEAD_DIM = 64
PAIRS = HEADS // 2
LANES = 2 * HEAD_DIM
SLABS = 4
SLAB = HEADS * HEAD_DIM // SLABS
VMEM = pl.BlockSpec(memory_space=pltpu.VMEM)


def first_head(shape):
    return lax.broadcasted_iota(jnp.int32, shape, len(shape) - 1) < HEAD_DIM


def lanes_of(p):
    return slice(p * LANES, (p + 1) * LANES)


def rows_of(p):
    return slice(p * HEAD_DIM, (p + 1) * HEAD_DIM)


def states_kernel(k_hbm, v_hbm, *refs):
    *outs, k_ref, v_ref, states, arrived = refs
    copies = []
    for s in range(SLABS):
        lanes = slice(s * SLAB, (s + 1) * SLAB)
        copies.append([
            pltpu.make_async_copy(k_hbm.at[:, lanes], k_ref.at[:, lanes], arrived.at[0, s]),
            pltpu.make_async_copy(v_hbm.at[:, lanes], v_ref.at[:, lanes], arrived.at[1, s])])
        for copy in copies[-1]:
            copy.start()
    first = first_head((HEAD_DIM, LANES))
    share = states.shape[1]
    for p in range(PAIRS):
        if p * LANES % SLAB == 0:
            for copy in copies[p * LANES // SLAB]:
                copy.wait()
        both = lax.dot_general(
            k_ref[:, lanes_of(p)], v_ref[:, lanes_of(p)], (((0,), (0,)), ((), ())),
            preferred_element_type=jnp.float32)
        packed = jnp.where(first, both[:HEAD_DIM], both[HEAD_DIM:])
        for j in range(HEAD_DIM // share):
            states[p * HEAD_DIM // share + j] = packed[j * share:(j + 1) * share]
    me = member()
    for d, out in enumerate(outs):
        out[...] = states[me ^ d]


def member():
    return lax.axis_index("chain") * lax.axis_size("inner") + lax.axis_index("inner")


def totals_kernel(inner, *refs):
    *parts, out_ref = refs
    for c in range(out_ref.shape[0]):
        total = parts[c * inner][...]
        for i in range(1, inner):
            total = total + parts[c * inner + i][...]
        out_ref[c] = total.astype(out_ref.dtype)


def prefix_kernel(inner, members, planes, *refs):
    parts, totals = refs[:members], refs[members:members + planes]
    outs, (order, sums, done) = refs[members + planes:-3], refs[-3:]
    me, chain, plane = member(), lax.axis_index("chain"), lax.axis_index("outer")
    chains = members // inner
    for d in range(members):
        order[me ^ d] = parts[d][...]
    shape = order.shape[1:]
    for c in range(chains):
        below = jnp.zeros(shape, jnp.float32)
        whole = jnp.zeros(shape, jnp.float32)
        for e in range(planes):
            there = totals[e][c].astype(jnp.float32)
            below = below + jnp.where((plane ^ e) < plane, there, 0.0)
            whole = whole + there
        sums[0, chain ^ c] = below
        sums[1, chain ^ c] = whole
    groups = jnp.zeros(shape, jnp.float32)
    for c in range(chains):
        total = groups + sums[0, c]
        groups = groups + sums[1, c]
        for i in range(inner):
            done[c * inner + i] = total
            if i < inner - 1:
                total = total + order[c * inner + i]
    for d, out in enumerate(outs):
        out[...] = done[me ^ d].astype(out.dtype)


def intra_kernel(q_ref, k_ref, v_ref, out_ref):
    rows = q_ref.shape[0]
    causal = (lax.broadcasted_iota(jnp.int32, (rows, rows), 0)
              >= lax.broadcasted_iota(jnp.int32, (rows, rows), 1))
    first = first_head((rows, LANES))
    zero = jnp.zeros((), jnp.bfloat16)
    for p in range(PAIRS):
        q, k, v = q_ref[:, lanes_of(p)], k_ref[:, lanes_of(p)], v_ref[:, lanes_of(p)]
        intra = []
        for mine in (first, ~first):
            scores = lax.dot_general(
                jnp.where(mine, q, zero), k, (((1,), (1,)), ((), ())),
                preferred_element_type=jnp.float32)
            scores = jnp.where(causal, scores, 0.0).astype(jnp.bfloat16)
            intra.append(jnp.dot(scores, v, preferred_element_type=jnp.float32))
        out_ref[:, lanes_of(p)] = jnp.where(first, intra[0], intra[1])


def attend_kernel(q_ref, intra_ref, *refs):
    *parts, out_ref, order = refs
    me = member()
    for d, part in enumerate(parts):
        order[me ^ d] = part[...]
    share = order.shape[1]
    first_state = first_head((HEAD_DIM, LANES))
    same = (first_head((LANES, LANES))
            == (lax.broadcasted_iota(jnp.int32, (LANES, LANES), 0) < HEAD_DIM))
    ones = jnp.where(same, 1.0, 0.0).astype(jnp.bfloat16)
    zero = jnp.zeros((), jnp.bfloat16)
    for p in range(PAIRS):
        packed = jnp.concatenate(
            [order[j] for j in range(p * HEAD_DIM // share, (p + 1) * HEAD_DIM // share)], axis=0)
        prefix = jnp.concatenate(
            [jnp.where(first_state, packed, zero), jnp.where(first_state, zero, packed)], axis=0)
        inter = jnp.dot(q_ref[:, lanes_of(p)], prefix, preferred_element_type=jnp.float32)
        total = intra_ref[:, lanes_of(p)] + inter
        square = total * total
        high = square.astype(jnp.bfloat16)
        low = (square - high.astype(jnp.float32)).astype(jnp.bfloat16)
        sums = (jnp.dot(high, ones, preferred_element_type=jnp.float32)
                + jnp.dot(low, ones, preferred_element_type=jnp.float32))
        out_ref[:, lanes_of(p)] = (total * lax.rsqrt(sums * (1.0 / HEAD_DIM) + 1e-6)).astype(out_ref.dtype)


def call(kernel, outs, *args, flops=0, scratch=(), memory=pltpu.VMEM):
    moved = sum(a.size * a.dtype.itemsize for a in args)
    single = not isinstance(outs, list)
    outs = [pltpu.VMEM(shape, dtype) for shape, dtype in ([outs] if single else outs)]
    args = [pltpu.with_memory_space_constraint(a, memory) for a in args]
    got = pl.pallas_call(
        kernel,
        out_shape=outs,
        in_specs=[pl.BlockSpec(memory_space=memory)] * len(args),
        out_specs=[VMEM] * len(outs),
        scratch_shapes=scratch,
        cost_estimate=pl.CostEstimate(flops=flops, bytes_accessed=moved, transcendentals=0),
        compiler_params=pltpu.CompilerParams(vmem_limit_bytes=16 * 1024 * 1024),
    )(*args)
    return got[0] if single else got


def swapped_outer(x, planes, e):
    return lax.ppermute(x, "outer", [(z, z ^ e) for z in range(planes)])


def swapped_plane(x, chains, inner, d):
    across, along = divmod(d, inner)
    return lax.ppermute(x, ("inner", "chain"), [
        (i * chains + c, (i ^ along) * chains + (c ^ across)) for i in range(inner) for c in range(chains)])


def per_device(chains, planes, inner, queries, keys, values):
    rows = queries.shape[0]
    members = chains * inner
    share = (PAIRS * HEAD_DIM // members, LANES)
    *states, keys, values = call(
        states_kernel,
        [(share, jnp.float32)] * members + [(keys.shape, keys.dtype), (values.shape, values.dtype)],
        keys, values, flops=2 * rows * LANES * LANES * PAIRS, memory=pltpu.HBM,
        scratch=[pltpu.VMEM((members,) + share, jnp.float32), pltpu.SemaphoreType.DMA((2, SLABS))])
    mine = [states[0]] + [swapped_plane(states[d], chains, inner, d) for d in range(1, members)]
    total = call(functools.partial(totals_kernel, inner), ((chains,) + share, jnp.bfloat16), *mine)
    totals = [total] + [swapped_outer(total, planes, e) for e in range(1, planes)]
    before = call(
        functools.partial(prefix_kernel, inner, members, planes), [(share, jnp.bfloat16)] * members,
        *mine, *totals,
        scratch=[pltpu.VMEM((members,) + share, jnp.float32), pltpu.VMEM((2, chains) + share, jnp.float32),
                 pltpu.VMEM((members,) + share, jnp.float32)])
    prefix = [before[0]] + [swapped_plane(before[d], chains, inner, d) for d in range(1, members)]
    intra = call(intra_kernel, (queries.shape, jnp.float32), queries, keys, values,
                 flops=4 * rows * rows * HEADS * HEAD_DIM)
    return pl.pallas_call(
        attend_kernel,
        out_shape=jax.ShapeDtypeStruct(queries.shape, jnp.bfloat16),
        in_specs=[VMEM] * (2 + members),
        out_specs=VMEM,
        scratch_shapes=[pltpu.VMEM((members,) + share, jnp.bfloat16)],
        compiler_params=pltpu.CompilerParams(vmem_limit_bytes=16 * 1024 * 1024),
    )(queries, intra, *prefix)


def solution(mesh):
    wide, chains = mesh.devices.shape
    inner = 4
    planes = wide // inner
    finer = jax.sharding.Mesh(mesh.devices.reshape(planes, inner, chains), ("outer", "inner", "chain"))
    spec = P(("chain", "outer", "inner"), None)
    return jax.shard_map(
        functools.partial(per_device, chains, planes, inner),
        mesh=finer,
        in_specs=(spec, spec, spec),
        out_specs=spec,
        check_vma=False,
    )
```

```python
import functools

import jax
import jax.numpy as jnp
from jax import lax
from jax.experimental import pallas as pl
from jax.experimental.pallas import tpu as pltpu
from jax.sharding import PartitionSpec as P

HEADS = 16
HEAD_DIM = 64
PAIRS = HEADS // 2
LANES = 2 * HEAD_DIM
SLABS = 4
SLAB = HEADS * HEAD_DIM // SLABS
VMEM = pl.BlockSpec(memory_space=pltpu.VMEM)


def first_head(shape):
    return lax.broadcasted_iota(jnp.int32, shape, len(shape) - 1) < HEAD_DIM


def lanes_of(p):
    return slice(p * LANES, (p + 1) * LANES)


def rows_of(p):
    return slice(p * HEAD_DIM, (p + 1) * HEAD_DIM)


def states_kernel(k_hbm, v_hbm, *refs):
    *outs, k_ref, v_ref, states, arrived = refs
    copies = []
    for s in range(SLABS):
        lanes = slice(s * SLAB, (s + 1) * SLAB)
        copies.append([
            pltpu.make_async_copy(k_hbm.at[:, lanes], k_ref.at[:, lanes], arrived.at[0, s]),
            pltpu.make_async_copy(v_hbm.at[:, lanes], v_ref.at[:, lanes], arrived.at[1, s])])
        for copy in copies[-1]:
            copy.start()
    first = first_head((HEAD_DIM, LANES))
    share = states.shape[1]
    for p in range(PAIRS):
        if p * LANES % SLAB == 0:
            for copy in copies[p * LANES // SLAB]:
                copy.wait()
        both = lax.dot_general(
            k_ref[:, lanes_of(p)], v_ref[:, lanes_of(p)], (((0,), (0,)), ((), ())),
            preferred_element_type=jnp.float32)
        packed = jnp.where(first, both[:HEAD_DIM], both[HEAD_DIM:])
        row = p * HEAD_DIM
        states[row // share, row % share:row % share + HEAD_DIM, :] = packed
    me = lax.axis_index("inner")
    for d, out in enumerate(outs):
        out[...] = states[me ^ d].astype(out.dtype)


def totals_kernel(*refs):
    *parts, out_ref, sent_ref = refs
    total = parts[0][...]
    for part in parts[1:]:
        total = total + part[...].astype(jnp.float32)
    out_ref[...] = total
    sent_ref[...] = total.astype(sent_ref.dtype)


def planes_kernel(*refs):
    *totals, below_ref, whole_ref = refs
    plane = lax.axis_index("outer")
    whole = totals[0][...]
    below = jnp.zeros_like(whole)
    for e, there in enumerate(totals[1:], 1):
        there = there[...].astype(jnp.float32)
        below = below + jnp.where((plane ^ e) < plane, there, 0.0)
        whole = whole + there
    below_ref[...] = below
    whole_ref[...] = whole


def prefix_kernel(*refs):
    inner = refs[-1].shape[0]
    parts, bases, outs, order = refs[:inner], refs[inner:-1 - inner], refs[-1 - inner:-1], refs[-1]
    me = lax.axis_index("inner")
    for d, part in enumerate(parts):
        order[me ^ d] = part[...].astype(jnp.float32)
    total = bases[0][...]
    for base in bases[1:]:
        total = total + base[...]
    for i in range(inner):
        here = order[i]
        order[i] = total
        total = total + here
    for d, out in enumerate(outs):
        out[...] = order[me ^ d].astype(out.dtype)


def intra_kernel(q_ref, k_ref, v_ref, out_ref):
    rows = q_ref.shape[0]
    causal = (lax.broadcasted_iota(jnp.int32, (rows, rows), 0)
              >= lax.broadcasted_iota(jnp.int32, (rows, rows), 1))
    first = first_head((rows, LANES))
    zero = jnp.zeros((), jnp.bfloat16)
    for p in range(PAIRS):
        q, k, v = q_ref[:, lanes_of(p)], k_ref[:, lanes_of(p)], v_ref[:, lanes_of(p)]
        intra = []
        for mine in (first, ~first):
            scores = lax.dot_general(
                jnp.where(mine, q, zero), k, (((1,), (1,)), ((), ())),
                preferred_element_type=jnp.float32)
            scores = jnp.where(causal, scores, 0.0).astype(jnp.bfloat16)
            intra.append(jnp.dot(scores, v, preferred_element_type=jnp.float32))
        out_ref[:, lanes_of(p)] = jnp.where(first, intra[0], intra[1])


def attend_kernel(q_ref, intra_ref, *refs):
    *parts, out_ref, order = refs
    me = lax.axis_index("inner")
    for d, part in enumerate(parts):
        order[me ^ d] = part[...]
    share = order.shape[1]
    first_state = first_head((HEAD_DIM, LANES))
    same = (first_head((LANES, LANES))
            == (lax.broadcasted_iota(jnp.int32, (LANES, LANES), 0) < HEAD_DIM))
    ones = jnp.where(same, 1.0, 0.0).astype(jnp.bfloat16)
    zero = jnp.zeros((), jnp.bfloat16)
    for p in range(PAIRS):
        row = p * HEAD_DIM
        packed = order[row // share, row % share:row % share + HEAD_DIM, :]
        prefix = jnp.concatenate(
            [jnp.where(first_state, packed, zero), jnp.where(first_state, zero, packed)], axis=0)
        inter = jnp.dot(q_ref[:, lanes_of(p)], prefix, preferred_element_type=jnp.float32)
        total = intra_ref[:, lanes_of(p)] + inter
        square = total * total
        high = square.astype(jnp.bfloat16)
        low = (square - high.astype(jnp.float32)).astype(jnp.bfloat16)
        sums = (jnp.dot(high, ones, preferred_element_type=jnp.float32)
                + jnp.dot(low, ones, preferred_element_type=jnp.float32))
        out_ref[:, lanes_of(p)] = (total * lax.rsqrt(sums * (1.0 / HEAD_DIM) + 1e-6)).astype(out_ref.dtype)


def call(kernel, outs, *args, flops=0, scratch=(), memory=pltpu.VMEM):
    moved = sum(a.size * a.dtype.itemsize for a in args)
    single = not isinstance(outs, list)
    outs = [pltpu.VMEM(shape, dtype) for shape, dtype in ([outs] if single else outs)]
    args = [pltpu.with_memory_space_constraint(a, memory) for a in args]
    got = pl.pallas_call(
        kernel,
        out_shape=outs,
        in_specs=[pl.BlockSpec(memory_space=memory)] * len(args),
        out_specs=[VMEM] * len(outs),
        scratch_shapes=scratch,
        cost_estimate=pl.CostEstimate(flops=flops, bytes_accessed=moved, transcendentals=0),
        compiler_params=pltpu.CompilerParams(vmem_limit_bytes=16 * 1024 * 1024),
    )(*args)
    return got[0] if single else got


def swapped(arrays, axis, own):
    size = len(arrays)
    got = {d: lax.ppermute(arrays[d], axis, [(i, i ^ d) for i in range(size)]) for d in reversed(range(1, size))}
    return [own] + [got[d] for d in range(1, size)]


def per_device(chains, planes, inner, queries, keys, values):
    rows = queries.shape[0]
    share = (PAIRS * HEAD_DIM // inner, LANES)
    own, *states, keys, values = call(
        states_kernel,
        [(share, jnp.float32)] + [(share, jnp.bfloat16)] * (inner - 1)
        + [(keys.shape, keys.dtype), (values.shape, values.dtype)],
        keys, values, flops=2 * rows * LANES * LANES * PAIRS, memory=pltpu.HBM,
        scratch=[pltpu.VMEM((inner,) + share, jnp.float32), pltpu.SemaphoreType.DMA((2, SLABS))])
    mine = swapped([own] + states, "inner", own)
    total, sent = call(totals_kernel, [(share, jnp.float32), (share, jnp.bfloat16)], *mine)
    totals = swapped([sent] * planes, "outer", total)
    below, whole = call(planes_kernel, [(share, jnp.float32)] * 2, *totals)
    groups = [lax.ppermute(whole, "chain", [(c, c + s) for c in range(chains - s)]) for s in range(1, chains)]
    before = call(prefix_kernel, [(share, jnp.bfloat16)] * inner, *mine, below, *groups,
                  scratch=[pltpu.VMEM((inner,) + share, jnp.float32)])
    prefix = swapped(before, "inner", before[0])
    intra = call(intra_kernel, (queries.shape, jnp.float32), queries, keys, values,
                 flops=4 * rows * rows * HEADS * HEAD_DIM)
    return pl.pallas_call(
        attend_kernel,
        out_shape=jax.ShapeDtypeStruct(queries.shape, jnp.bfloat16),
        in_specs=[VMEM] * (2 + inner),
        out_specs=VMEM,
        scratch_shapes=[pltpu.VMEM((inner,) + share, jnp.bfloat16)],
        compiler_params=pltpu.CompilerParams(vmem_limit_bytes=16 * 1024 * 1024),
    )(queries, intra, *prefix)


def solution(mesh):
    wide, chains = mesh.devices.shape
    inner = 4
    planes = wide // inner
    finer = jax.sharding.Mesh(mesh.devices.reshape(planes, inner, chains), ("outer", "inner", "chain"))
    spec = P(("chain", "outer", "inner"), None)
    return jax.shard_map(
        functools.partial(per_device, chains, planes, inner),
        mesh=finer,
        in_specs=(spec, spec, spec),
        out_specs=spec,
        check_vma=False,
    )
```

```python
import functools

import jax
import jax.numpy as jnp
from jax import lax
from jax.experimental import pallas as pl
from jax.experimental.pallas import tpu as pltpu
from jax.sharding import PartitionSpec as P

HEADS = 16
HEAD_DIM = 64
PAIRS = HEADS // 2
LANES = 2 * HEAD_DIM
AXES = ("chain", "wide")
CHUNKS = 4
SLAB = 256
VMEM = pl.BlockSpec(memory_space=pltpu.VMEM)
BF16 = jnp.bfloat16
F32 = jnp.float32


def first_head(shape):
    return lax.broadcasted_iota(jnp.int32, shape, len(shape) - 1) < HEAD_DIM


def lanes_of(p):
    return slice(p * LANES, (p + 1) * LANES)


def rows_of(p):
    return slice(p * HEAD_DIM, (p + 1) * HEAD_DIM)


def states_kernel(k_hbm, v_hbm, out_ref, k_ref, v_ref, sums, arrived):
    rows = k_ref.shape[0] // CHUNKS
    copies = []
    for s in range(CHUNKS):
        chunk = pl.ds(s * rows, rows)
        copies.append([
            pltpu.make_async_copy(k_hbm.at[chunk], k_ref.at[chunk], arrived.at[0, s]),
            pltpu.make_async_copy(v_hbm.at[chunk], v_ref.at[chunk], arrived.at[1, s])])
        for copy in copies[-1]:
            copy.start()
    first = first_head((HEAD_DIM, LANES))
    for s in range(CHUNKS):
        for copy in copies[s]:
            copy.wait()
        chunk = slice(s * rows, (s + 1) * rows)
        for p in range(PAIRS):
            both = lax.dot_general(
                k_ref[chunk, lanes_of(p)], v_ref[chunk, lanes_of(p)], (((0,), (0,)), ((), ())),
                preferred_element_type=F32)
            packed = jnp.where(first, both[:HEAD_DIM], both[HEAD_DIM:])
            if s > 0:
                packed = sums[rows_of(p), :] + packed
            if s < CHUNKS - 1:
                sums[rows_of(p), :] = packed
            else:
                out_ref[rows_of(p), :] = packed.astype(out_ref.dtype)


def scan_kernel(x_ref, out_ref):
    parts = x_ref.shape[0]
    total = jnp.zeros(x_ref.shape[1:], F32)
    for i in range(parts):
        out_ref[i] = total.astype(out_ref.dtype)
        if i < parts - 1:
            total = total + x_ref[i].astype(F32)


def scan_rows_kernel(x_ref, out_ref):
    parts = x_ref.shape[0]
    row = lax.broadcasted_iota(jnp.int32, (parts, parts), 0)
    col = lax.broadcasted_iota(jnp.int32, (parts, parts), 1)
    below = jnp.where(col < row, 1.0, 0.0).astype(BF16)
    out_ref[...] = jnp.dot(below, x_ref[...], preferred_element_type=F32).astype(out_ref.dtype)


def intra_kernel(q_ref, k_ref, v_ref, out_ref):
    rows = q_ref.shape[0]
    causal = (lax.broadcasted_iota(jnp.int32, (rows, rows), 0)
              >= lax.broadcasted_iota(jnp.int32, (rows, rows), 1))
    first = first_head((rows, LANES))
    zero = jnp.zeros((), BF16)
    for p in range(PAIRS):
        q, k, v = q_ref[:, lanes_of(p)], k_ref[:, lanes_of(p)], v_ref[:, lanes_of(p)]
        intra = []
        for mine in (first, ~first):
            scores = lax.dot_general(
                jnp.where(mine, q, zero), k, (((1,), (1,)), ((), ())),
                preferred_element_type=F32)
            scores = jnp.where(causal, scores, 0.0).astype(BF16)
            intra.append(jnp.dot(scores, v, preferred_element_type=F32))
        out_ref[:, lanes_of(p)] = jnp.where(first, intra[0], intra[1])


def attend_kernel(q_ref, intra_ref, prefix_ref, out_hbm, out_ref, sent):
    heads = SLAB // HEAD_DIM
    blocks = ([lax.broadcasted_iota(jnp.int32, (SLAB, SLAB), d) // HEAD_DIM for d in range(2)])
    same = blocks[0] == blocks[1]
    ones = jnp.where(same, 1.0, 0.0).astype(BF16)
    zero = jnp.zeros((), BF16)
    copies = []
    for s in range(HEADS // heads):
        lanes = slice(s * SLAB, (s + 1) * SLAB)
        rows = []
        for p in range(s * heads // 2, (s + 1) * heads // 2):
            rows += [jnp.concatenate([prefix_ref[rows_of(p), :]] * (SLAB // LANES), axis=1)] * 2
        prefix = jnp.where(same, jnp.concatenate(rows, axis=0), zero)
        inter = jnp.dot(q_ref[:, lanes], prefix, preferred_element_type=F32)
        total = intra_ref[:, lanes] + inter
        square = total * total
        high = square.astype(BF16)
        low = (square - high.astype(F32)).astype(BF16)
        sums = (jnp.dot(high, ones, preferred_element_type=F32)
                + jnp.dot(low, ones, preferred_element_type=F32))
        out_ref[:, lanes] = (total * lax.rsqrt(sums * (1.0 / HEAD_DIM) + 1e-6)).astype(out_ref.dtype)
        copies.append(pltpu.make_async_copy(out_ref.at[:, lanes], out_hbm.at[:, lanes], sent.at[s]))
        copies[-1].start()
    for copy in copies:
        copy.wait()


def call(kernel, outs, *args, flops=0, scratch=(), source=pltpu.VMEM, result=pltpu.VMEM):
    moved = sum(a.size * a.dtype.itemsize for a in args)
    single = not isinstance(outs, list)
    outs = [outs] if single else outs
    got = pl.pallas_call(
        kernel,
        out_shape=[result(shape, dtype) for shape, dtype in outs],
        in_specs=[pl.BlockSpec(memory_space=source)] * len(args),
        out_specs=[pl.BlockSpec(memory_space=result)] * len(outs),
        scratch_shapes=scratch,
        cost_estimate=pl.CostEstimate(flops=flops, bytes_accessed=moved, transcendentals=0),
        compiler_params=pltpu.CompilerParams(vmem_limit_bytes=16 * 1024 * 1024),
    )(*[pltpu.with_memory_space_constraint(a, source) for a in args])
    return got[0] if single else got


def per_device(parts, queries, keys, values):
    rows = queries.shape[0]
    state = (PAIRS * HEAD_DIM, LANES)
    share = state[0] // parts
    states, keys, values = call(
        states_kernel, [(state, BF16), (keys.shape, keys.dtype), (values.shape, values.dtype)],
        keys, values, flops=2 * rows * LANES * LANES * PAIRS, source=pltpu.HBM,
        scratch=[pltpu.VMEM(state, F32), pltpu.SemaphoreType.DMA((2, CHUNKS))])
    view = (parts, share, LANES) if share > 1 else (parts, LANES)
    mine = lax.all_to_all(states.reshape(view), AXES, 0, 0, tiled=True)
    mine, queries = lax.optimization_barrier((mine, queries))
    before = call(scan_kernel if share > 1 else scan_rows_kernel, (view, BF16), mine)
    prefix = lax.all_to_all(before, AXES, 0, 0, tiled=True).reshape(state)
    intra = call(intra_kernel, (queries.shape, F32), queries, keys, values,
                 flops=4 * rows * rows * HEADS * HEAD_DIM)
    return call(attend_kernel, (queries.shape, BF16), queries, intra, prefix, result=pltpu.HBM,
                flops=2 * rows * SLAB * HEADS * HEAD_DIM,
                scratch=[pltpu.VMEM(queries.shape, BF16), pltpu.SemaphoreType.DMA((HEADS * HEAD_DIM // SLAB,))])


def solution(mesh):
    spec = P(AXES, None)
    parts = mesh.shape["chain"] * mesh.shape["wide"]
    return jax.shard_map(
        functools.partial(per_device, parts),
        mesh=mesh,
        in_specs=(spec, spec, spec),
        out_specs=spec,
        check_vma=False,
    )
```

```python
import functools

import jax
import jax.numpy as jnp
from jax import lax
from jax.experimental import pallas as pl
from jax.experimental.pallas import tpu as pltpu
from jax.sharding import PartitionSpec as P

HEADS = 16
HEAD_DIM = 64
PAIRS = HEADS // 2
LANES = 2 * HEAD_DIM
AXES = ("chain", "wide")
CHUNKS = 4
SLAB = 256
VMEM = pl.BlockSpec(memory_space=pltpu.VMEM)
BF16 = jnp.bfloat16
F32 = jnp.float32


def first_head(shape):
    return lax.broadcasted_iota(jnp.int32, shape, len(shape) - 1) < HEAD_DIM


def lanes_of(p):
    return slice(p * LANES, (p + 1) * LANES)


def rows_of(p):
    return slice(p * HEAD_DIM, (p + 1) * HEAD_DIM)


def states_kernel(k_hbm, v_hbm, out_ref, k_ref, v_ref, sums, arrived):
    rows = k_ref.shape[0] // CHUNKS
    copies = []
    for s in range(CHUNKS):
        chunk = pl.ds(s * rows, rows)
        copies.append([
            pltpu.make_async_copy(k_hbm.at[chunk], k_ref.at[chunk], arrived.at[0, s]),
            pltpu.make_async_copy(v_hbm.at[chunk], v_ref.at[chunk], arrived.at[1, s])])
        for copy in copies[-1]:
            copy.start()
    first = first_head((HEAD_DIM, LANES))
    for s in range(CHUNKS):
        for copy in copies[s]:
            copy.wait()
        chunk = slice(s * rows, (s + 1) * rows)
        for p in range(PAIRS):
            both = lax.dot_general(
                k_ref[chunk, lanes_of(p)], v_ref[chunk, lanes_of(p)], (((0,), (0,)), ((), ())),
                preferred_element_type=F32)
            packed = jnp.where(first, both[:HEAD_DIM], both[HEAD_DIM:])
            if s > 0:
                packed = sums[rows_of(p), :] + packed
            if s < CHUNKS - 1:
                sums[rows_of(p), :] = packed
            else:
                out_ref[rows_of(p), :] = packed.astype(out_ref.dtype)


def totals_kernel(x_ref, out_ref):
    total = x_ref[0].astype(F32)
    for i in range(1, x_ref.shape[0]):
        total = total + x_ref[i].astype(F32)
    out_ref[...] = total


def scan_kernel(x_ref, *refs):
    *groups, out_ref = refs
    chain = lax.axis_index("chain")
    total = jnp.zeros(x_ref.shape[1:], F32)
    for d, group in enumerate(groups, 1):
        total = total + jnp.where((chain ^ d) < chain, group[...], 0.0)
    for i in reversed(range(x_ref.shape[0])):
        out_ref[i] = total.astype(out_ref.dtype)
        total = total + x_ref[i].astype(F32)


def intra_kernel(q_ref, k_ref, v_ref, out_ref):
    rows = q_ref.shape[0]
    causal = (lax.broadcasted_iota(jnp.int32, (rows, rows), 0)
              >= lax.broadcasted_iota(jnp.int32, (rows, rows), 1))
    first = first_head((rows, LANES))
    zero = jnp.zeros((), BF16)
    for p in range(PAIRS):
        q, k, v = q_ref[:, lanes_of(p)], k_ref[:, lanes_of(p)], v_ref[:, lanes_of(p)]
        intra = []
        for mine in (first, ~first):
            scores = lax.dot_general(
                jnp.where(mine, q, zero), k, (((1,), (1,)), ((), ())),
                preferred_element_type=F32)
            scores = jnp.where(causal, scores, 0.0).astype(BF16)
            intra.append(jnp.dot(scores, v, preferred_element_type=F32))
        out_ref[:, lanes_of(p)] = jnp.where(first, intra[0], intra[1])


def attend_kernel(q_ref, intra_ref, prefix_ref, out_hbm, out_ref, sent):
    heads = SLAB // HEAD_DIM
    blocks = ([lax.broadcasted_iota(jnp.int32, (SLAB, SLAB), d) // HEAD_DIM for d in range(2)])
    same = blocks[0] == blocks[1]
    ones = jnp.where(same, 1.0, 0.0).astype(BF16)
    zero = jnp.zeros((), BF16)
    copies = []
    for s in range(HEADS // heads):
        lanes = slice(s * SLAB, (s + 1) * SLAB)
        rows = []
        for p in range(s * heads // 2, (s + 1) * heads // 2):
            rows += [jnp.concatenate([prefix_ref[rows_of(p), :]] * (SLAB // LANES), axis=1)] * 2
        prefix = jnp.where(same, jnp.concatenate(rows, axis=0), zero)
        inter = jnp.dot(q_ref[:, lanes], prefix, preferred_element_type=F32)
        total = intra_ref[:, lanes] + inter
        square = total * total
        high = square.astype(BF16)
        low = (square - high.astype(F32)).astype(BF16)
        sums = (jnp.dot(high, ones, preferred_element_type=F32)
                + jnp.dot(low, ones, preferred_element_type=F32))
        out_ref[:, lanes] = (total * lax.rsqrt(sums * (1.0 / HEAD_DIM) + 1e-6)).astype(out_ref.dtype)
        copies.append(pltpu.make_async_copy(out_ref.at[:, lanes], out_hbm.at[:, lanes], sent.at[s]))
        copies[-1].start()
    for copy in copies:
        copy.wait()


def call(kernel, outs, *args, flops=0, scratch=(), source=pltpu.VMEM, result=pltpu.VMEM):
    moved = sum(a.size * a.dtype.itemsize for a in args)
    single = not isinstance(outs, list)
    outs = [outs] if single else outs
    got = pl.pallas_call(
        kernel,
        out_shape=[result(shape, dtype) for shape, dtype in outs],
        in_specs=[pl.BlockSpec(memory_space=source)] * len(args),
        out_specs=[pl.BlockSpec(memory_space=result)] * len(outs),
        scratch_shapes=scratch,
        cost_estimate=pl.CostEstimate(flops=flops, bytes_accessed=moved, transcendentals=0),
        compiler_params=pltpu.CompilerParams(vmem_limit_bytes=16 * 1024 * 1024),
    )(*[pltpu.with_memory_space_constraint(a, source) for a in args])
    return got[0] if single else got


def per_device(chains, wide, queries, keys, values):
    rows = queries.shape[0]
    state = (PAIRS * HEAD_DIM, LANES)
    share = state[0] // wide
    states, keys, values = call(
        states_kernel, [(state, BF16), (keys.shape, keys.dtype), (values.shape, values.dtype)],
        keys, values, flops=2 * rows * LANES * LANES * PAIRS, source=pltpu.HBM,
        scratch=[pltpu.VMEM(state, F32), pltpu.SemaphoreType.DMA((2, CHUNKS))])
    view = (wide, share, LANES)
    order = [list(reversed(range(wide)))]
    mine = lax.all_to_all(states.reshape(view), "wide", 0, 0, axis_index_groups=order, tiled=True)
    mine, queries = lax.optimization_barrier((mine, queries))
    total = call(totals_kernel, (view[1:], F32), mine)
    groups = [lax.ppermute(total, "chain", [(c, c ^ d) for c in range(chains)]) for d in range(1, chains)]
    before = call(scan_kernel, (view, BF16), mine, *groups)
    prefix = lax.all_to_all(before, "wide", 0, 0, axis_index_groups=order, tiled=True).reshape(state)
    intra = call(intra_kernel, (queries.shape, F32), queries, keys, values,
                 flops=4 * rows * rows * HEADS * HEAD_DIM)
    return call(attend_kernel, (queries.shape, BF16), queries, intra, prefix, result=pltpu.HBM,
                flops=2 * rows * SLAB * HEADS * HEAD_DIM,
                scratch=[pltpu.VMEM(queries.shape, BF16), pltpu.SemaphoreType.DMA((HEADS * HEAD_DIM // SLAB,))])


def solution(mesh):
    spec = P(AXES, None)
    return jax.shard_map(
        functools.partial(per_device, mesh.shape["chain"], mesh.shape["wide"]),
        mesh=mesh,
        in_specs=(spec, spec, spec),
        out_specs=spec,
        check_vma=False,
    )
```

```python
import functools

import jax
import jax.numpy as jnp
from jax import lax
from jax.experimental import pallas as pl
from jax.experimental.pallas import tpu as pltpu
from jax.sharding import PartitionSpec as P

HEADS = 16
HEAD_DIM = 64
PAIRS = HEADS // 2
LANES = 2 * HEAD_DIM
AXES = ("chain", "wide")
CHUNKS = 4
SLAB = 256
VMEM = pl.BlockSpec(memory_space=pltpu.VMEM)
BF16 = jnp.bfloat16
F32 = jnp.float32


def first_head(shape):
    return lax.broadcasted_iota(jnp.int32, shape, len(shape) - 1) < HEAD_DIM


def lanes_of(p):
    return slice(p * LANES, (p + 1) * LANES)


def rows_of(p):
    return slice(p * HEAD_DIM, (p + 1) * HEAD_DIM)


def states_kernel(places, k_hbm, v_hbm, out_ref, k_ref, v_ref, sums, arrived):
    share = out_ref.shape[0] // len(places)
    moved = places != list(range(len(places)))
    rows = k_ref.shape[0] // CHUNKS
    copies = []
    for s in range(CHUNKS):
        chunk = pl.ds(s * rows, rows)
        copies.append([
            pltpu.make_async_copy(k_hbm.at[chunk], k_ref.at[chunk], arrived.at[0, s]),
            pltpu.make_async_copy(v_hbm.at[chunk], v_ref.at[chunk], arrived.at[1, s])])
        for copy in copies[-1]:
            copy.start()
    first = first_head((HEAD_DIM, LANES))
    for s in range(CHUNKS):
        for copy in copies[s]:
            copy.wait()
        chunk = slice(s * rows, (s + 1) * rows)
        for p in range(PAIRS):
            both = lax.dot_general(
                k_ref[chunk, lanes_of(p)], v_ref[chunk, lanes_of(p)], (((0,), (0,)), ((), ())),
                preferred_element_type=F32)
            packed = jnp.where(first, both[:HEAD_DIM], both[HEAD_DIM:])
            if s > 0:
                packed = sums[rows_of(p), :] + packed
            if s < CHUNKS - 1:
                sums[rows_of(p), :] = packed
            elif not moved:
                out_ref[rows_of(p), :] = packed.astype(out_ref.dtype)
            else:
                for j in range(HEAD_DIM // share):
                    place = places[p * HEAD_DIM // share + j] * share
                    out_ref[place:place + share, :] = packed[j * share:(j + 1) * share].astype(out_ref.dtype)


def scan_kernel(order, leads, x_ref, out_ref):
    parts = x_ref.shape[0]
    total = jnp.zeros(x_ref.shape[1:], F32)
    for i in range(parts):
        out_ref[leads[i]] = total.astype(out_ref.dtype)
        if i < parts - 1:
            total = total + x_ref[order[i]].astype(F32)


def intra_kernel(q_ref, k_ref, v_ref, out_ref):
    rows = q_ref.shape[0]
    causal = (lax.broadcasted_iota(jnp.int32, (rows, rows), 0)
              >= lax.broadcasted_iota(jnp.int32, (rows, rows), 1))
    first = first_head((rows, LANES))
    zero = jnp.zeros((), BF16)
    for p in range(PAIRS):
        q, k, v = q_ref[:, lanes_of(p)], k_ref[:, lanes_of(p)], v_ref[:, lanes_of(p)]
        intra = []
        for mine in (first, ~first):
            scores = lax.dot_general(
                jnp.where(mine, q, zero), k, (((1,), (1,)), ((), ())),
                preferred_element_type=F32)
            scores = jnp.where(causal, scores, 0.0).astype(BF16)
            intra.append(jnp.dot(scores, v, preferred_element_type=F32))
        out_ref[:, lanes_of(p)] = jnp.where(first, intra[0], intra[1])


def attend_kernel(q_ref, intra_ref, prefix_ref, out_hbm, out_ref, sent):
    heads = SLAB // HEAD_DIM
    blocks = ([lax.broadcasted_iota(jnp.int32, (SLAB, SLAB), d) // HEAD_DIM for d in range(2)])
    same = blocks[0] == blocks[1]
    ones = jnp.where(same, 1.0, 0.0).astype(BF16)
    zero = jnp.zeros((), BF16)
    copies = []
    for s in range(HEADS // heads):
        lanes = slice(s * SLAB, (s + 1) * SLAB)
        rows = []
        for p in range(s * heads // 2, (s + 1) * heads // 2):
            rows += [jnp.concatenate([prefix_ref[rows_of(p), :]] * (SLAB // LANES), axis=1)] * 2
        prefix = jnp.where(same, jnp.concatenate(rows, axis=0), zero)
        inter = jnp.dot(q_ref[:, lanes], prefix, preferred_element_type=F32)
        total = intra_ref[:, lanes] + inter
        square = total * total
        high = square.astype(BF16)
        low = (square - high.astype(F32)).astype(BF16)
        sums = (jnp.dot(high, ones, preferred_element_type=F32)
                + jnp.dot(low, ones, preferred_element_type=F32))
        out_ref[:, lanes] = (total * lax.rsqrt(sums * (1.0 / HEAD_DIM) + 1e-6)).astype(out_ref.dtype)
        copies.append(pltpu.make_async_copy(out_ref.at[:, lanes], out_hbm.at[:, lanes], sent.at[s]))
        copies[-1].start()
    for copy in copies:
        copy.wait()


def call(kernel, outs, *args, flops=0, scratch=(), source=pltpu.VMEM, result=pltpu.VMEM):
    moved = sum(a.size * a.dtype.itemsize for a in args)
    single = not isinstance(outs, list)
    outs = [outs] if single else outs
    got = pl.pallas_call(
        kernel,
        out_shape=[result(shape, dtype) for shape, dtype in outs],
        in_specs=[pl.BlockSpec(memory_space=source)] * len(args),
        out_specs=[pl.BlockSpec(memory_space=result)] * len(outs),
        scratch_shapes=scratch,
        cost_estimate=pl.CostEstimate(flops=flops, bytes_accessed=moved, transcendentals=0),
        compiler_params=pltpu.CompilerParams(vmem_limit_bytes=16 * 1024 * 1024),
    )(*[pltpu.with_memory_space_constraint(a, source) for a in args])
    return got[0] if single else got


def led_by(parts, first):
    order = list(range(parts))
    order[0], order[first] = first, 0
    return order


def per_device(wide, parts, queries, keys, values):
    rows = queries.shape[0]
    state = (PAIRS * HEAD_DIM, LANES)
    share = state[0] // parts
    first = led_by(parts, parts - 1)
    second = led_by(parts, 3 * wide // 4 - 1) if share % 16 == 0 else first
    places = [first[second[s]] for s in range(parts)]
    states, keys, values = call(
        functools.partial(states_kernel, places), [(state, BF16), (keys.shape, keys.dtype), (values.shape, values.dtype)],
        keys, values, flops=2 * rows * LANES * LANES * PAIRS, source=pltpu.HBM,
        scratch=[pltpu.VMEM(state, F32), pltpu.SemaphoreType.DMA((2, CHUNKS))])
    view = (parts, share, LANES)
    mine = lax.all_to_all(states.reshape(view), AXES, 0, 0, axis_index_groups=[first], tiled=True)
    mine, queries = lax.optimization_barrier((mine, queries))
    before = call(functools.partial(scan_kernel, first, second), (view, BF16), mine)
    prefix = lax.all_to_all(before, AXES, 0, 0, axis_index_groups=[second], tiled=True).reshape(state)
    intra = call(intra_kernel, (queries.shape, F32), queries, keys, values,
                 flops=4 * rows * rows * HEADS * HEAD_DIM)
    return call(attend_kernel, (queries.shape, BF16), queries, intra, prefix, result=pltpu.HBM,
                flops=2 * rows * SLAB * HEADS * HEAD_DIM,
                scratch=[pltpu.VMEM(queries.shape, BF16), pltpu.SemaphoreType.DMA((HEADS * HEAD_DIM // SLAB,))])


def solution(mesh):
    spec = P(AXES, None)
    parts = mesh.shape["chain"] * mesh.shape["wide"]
    return jax.shard_map(
        functools.partial(per_device, mesh.shape["wide"], parts),
        mesh=mesh,
        in_specs=(spec, spec, spec),
        out_specs=spec,
        check_vma=False,
    )
```

```python
import functools

import jax
import jax.numpy as jnp
from jax import lax
from jax.experimental import pallas as pl
from jax.experimental.pallas import tpu as pltpu
from jax.sharding import PartitionSpec as P

HEADS = 16
HEAD_DIM = 64
PAIRS = HEADS // 2
LANES = 2 * HEAD_DIM
SLABS = 4
SLAB = 256
VMEM = pl.BlockSpec(memory_space=pltpu.VMEM)
BF16 = jnp.bfloat16
F32 = jnp.float32


def first_head(shape):
    return lax.broadcasted_iota(jnp.int32, shape, len(shape) - 1) < HEAD_DIM


def lanes_of(p):
    return slice(p * LANES, (p + 1) * LANES)


def rows_of(p):
    return slice(p * HEAD_DIM, (p + 1) * HEAD_DIM)


def states_kernel(k_hbm, v_hbm, *refs):
    *outs, k_ref, v_ref, states, arrived = refs
    copies = []
    for s in range(SLABS):
        lanes = slice(s * SLAB, (s + 1) * SLAB)
        copies.append([
            pltpu.make_async_copy(k_hbm.at[:, lanes], k_ref.at[:, lanes], arrived.at[0, s]),
            pltpu.make_async_copy(v_hbm.at[:, lanes], v_ref.at[:, lanes], arrived.at[1, s])])
        for copy in copies[-1]:
            copy.start()
    first = first_head((HEAD_DIM, LANES))
    share = states.shape[1]
    for p in range(PAIRS):
        if p * LANES % SLAB == 0:
            for copy in copies[p * LANES // SLAB]:
                copy.wait()
        both = lax.dot_general(
            k_ref[:, lanes_of(p)], v_ref[:, lanes_of(p)], (((0,), (0,)), ((), ())),
            preferred_element_type=jnp.float32)
        packed = jnp.where(first, both[:HEAD_DIM], both[HEAD_DIM:])
        row = p * HEAD_DIM
        states[row // share, row % share:row % share + HEAD_DIM, :] = packed
    me = lax.axis_index("inner")
    for d, out in enumerate(outs):
        out[...] = states[me ^ d].astype(out.dtype)


def totals_kernel(*refs):
    *parts, own, out_ref, sent_ref = refs
    total = own[...]
    for part in parts:
        total = total + part[...].astype(F32)
    out_ref[...] = total
    sent_ref[...] = total.astype(sent_ref.dtype)


def planes_kernel(*refs):
    *totals, own, below_ref, whole_ref = refs
    plane = lax.axis_index("outer")
    whole = own[...]
    below = jnp.zeros_like(whole)
    for e, there in zip(reversed(range(1, len(totals) + 1)), totals):
        there = there[...].astype(F32)
        below = below + jnp.where((plane ^ e) < plane, there, 0.0)
        whole = whole + there
    below_ref[...] = below
    whole_ref[...] = whole


def prefix_kernel(inner, *refs):
    *ins, order = refs
    parts, below, groups, outs = ins[:inner], ins[inner], ins[inner + 1:-inner], ins[-inner:]
    me, chain = lax.axis_index("inner"), lax.axis_index("chain")
    for d, part in zip(reversed(range(inner)), parts):
        order[me ^ d] = part[...].astype(F32)
    total = below[...]
    for d, group in enumerate(groups, 1):
        total = total + jnp.where((chain ^ d) < chain, group[...], 0.0)
    for i in range(inner):
        here = order[i]
        order[i] = total
        total = total + here
    for d, out in enumerate(outs):
        out[...] = order[me ^ d].astype(out.dtype)


def intra_kernel(q_ref, k_ref, v_ref, out_ref):
    rows = q_ref.shape[0]
    causal = (lax.broadcasted_iota(jnp.int32, (rows, rows), 0)
              >= lax.broadcasted_iota(jnp.int32, (rows, rows), 1))
    first = first_head((rows, LANES))
    zero = jnp.zeros((), BF16)
    for p in range(PAIRS):
        q, k, v = q_ref[:, lanes_of(p)], k_ref[:, lanes_of(p)], v_ref[:, lanes_of(p)]
        intra = []
        for mine in (first, ~first):
            scores = lax.dot_general(
                jnp.where(mine, q, zero), k, (((1,), (1,)), ((), ())),
                preferred_element_type=F32)
            scores = jnp.where(causal, scores, 0.0).astype(BF16)
            intra.append(jnp.dot(scores, v, preferred_element_type=F32))
        out_ref[:, lanes_of(p)] = jnp.where(first, intra[0], intra[1])


def attend_kernel(inner, q_ref, intra_ref, *refs):
    *parts, out_hbm, out_ref, prefix_ref, sent = refs
    me = lax.axis_index("inner")
    for d, part in zip(reversed(range(inner)), parts):
        prefix_ref[me ^ d] = part[...]
    share = prefix_ref.shape[1]
    heads = SLAB // HEAD_DIM
    blocks = ([lax.broadcasted_iota(jnp.int32, (SLAB, SLAB), d) // HEAD_DIM for d in range(2)])
    same = blocks[0] == blocks[1]
    ones = jnp.where(same, 1.0, 0.0).astype(BF16)
    zero = jnp.zeros((), BF16)
    copies = []
    for s in range(HEADS // heads):
        lanes = slice(s * SLAB, (s + 1) * SLAB)
        rows = []
        for p in range(s * heads // 2, (s + 1) * heads // 2):
            row = p * HEAD_DIM
            pair = prefix_ref[row // share, row % share:row % share + HEAD_DIM, :]
            rows += [jnp.concatenate([pair] * (SLAB // LANES), axis=1)] * 2
        prefix = jnp.where(same, jnp.concatenate(rows, axis=0), zero)
        inter = jnp.dot(q_ref[:, lanes], prefix, preferred_element_type=F32)
        total = intra_ref[:, lanes] + inter
        square = total * total
        high = square.astype(BF16)
        low = (square - high.astype(F32)).astype(BF16)
        sums = (jnp.dot(high, ones, preferred_element_type=F32)
                + jnp.dot(low, ones, preferred_element_type=F32))
        out_ref[:, lanes] = (total * lax.rsqrt(sums * (1.0 / HEAD_DIM) + 1e-6)).astype(out_ref.dtype)
        copies.append(pltpu.make_async_copy(out_ref.at[:, lanes], out_hbm.at[:, lanes], sent.at[s]))
        copies[-1].start()
    for copy in copies:
        copy.wait()


def call(kernel, outs, *args, flops=0, scratch=(), source=pltpu.VMEM, result=pltpu.VMEM):
    moved = sum(a.size * a.dtype.itemsize for a in args)
    single = not isinstance(outs, list)
    outs = [outs] if single else outs
    got = pl.pallas_call(
        kernel,
        out_shape=[result(shape, dtype) for shape, dtype in outs],
        in_specs=[pl.BlockSpec(memory_space=source)] * len(args),
        out_specs=[pl.BlockSpec(memory_space=result)] * len(outs),
        scratch_shapes=scratch,
        cost_estimate=pl.CostEstimate(flops=flops, bytes_accessed=moved, transcendentals=0),
        compiler_params=pltpu.CompilerParams(vmem_limit_bytes=16 * 1024 * 1024),
    )(*[pltpu.with_memory_space_constraint(a, source) for a in args])
    return got[0] if single else got


def swapped(arrays, axis, own):
    size = len(arrays)
    return [lax.ppermute(arrays[d], axis, [(i, i ^ d) for i in range(size)]) for d in reversed(range(1, size))] + [own]


def per_device(chains, planes, inner, queries, keys, values):
    rows = queries.shape[0]
    share = (PAIRS * HEAD_DIM // inner, LANES)
    own, *states, keys, values = call(
        states_kernel,
        [(share, F32)] + [(share, BF16)] * (inner - 1) + [(keys.shape, keys.dtype), (values.shape, values.dtype)],
        keys, values, flops=2 * rows * LANES * LANES * PAIRS, source=pltpu.HBM,
        scratch=[pltpu.VMEM((inner,) + share, F32), pltpu.SemaphoreType.DMA((2, SLABS))])
    mine = swapped([own] + states, "inner", own)
    total, sent = call(totals_kernel, [(share, F32), (share, BF16)], *mine)
    totals = swapped([sent] * planes, "outer", total)
    below, whole = call(planes_kernel, [(share, F32)] * 2, *totals)
    groups = [lax.ppermute(whole, "chain", [(c, c ^ d) for c in range(chains)]) for d in range(1, chains)]
    before = call(functools.partial(prefix_kernel, inner), [(share, BF16)] * inner, *mine, below, *groups,
                  scratch=[pltpu.VMEM((inner,) + share, F32)])
    prefix = swapped(before, "inner", before[0])
    intra = call(intra_kernel, (queries.shape, F32), queries, keys, values,
                 flops=4 * rows * rows * HEADS * HEAD_DIM)
    return call(functools.partial(attend_kernel, inner), (queries.shape, BF16), queries, intra, *prefix,
                result=pltpu.HBM, flops=2 * rows * SLAB * HEADS * HEAD_DIM,
                scratch=[pltpu.VMEM(queries.shape, BF16), pltpu.VMEM((inner,) + share, BF16),
                         pltpu.SemaphoreType.DMA((HEADS * HEAD_DIM // SLAB,))])


def solution(mesh):
    wide, chains = mesh.devices.shape
    inner = 4
    planes = wide // inner
    finer = jax.sharding.Mesh(mesh.devices.reshape(planes, inner, chains), ("outer", "inner", "chain"))
    spec = P(("chain", "outer", "inner"), None)
    return jax.shard_map(
        functools.partial(per_device, chains, planes, inner),
        mesh=finer,
        in_specs=(spec, spec, spec),
        out_specs=spec,
        check_vma=False,
    )
```

```python
import functools

import jax
import jax.numpy as jnp
from jax import lax
from jax.experimental import pallas as pl
from jax.experimental.pallas import tpu as pltpu
from jax.sharding import PartitionSpec as P

HEADS = 16
HEAD_DIM = 64
PAIRS = HEADS // 2
LANES = 2 * HEAD_DIM
SLABS = 4
SLAB = 256
VMEM = pl.BlockSpec(memory_space=pltpu.VMEM)
BF16 = jnp.bfloat16
F32 = jnp.float32


def first_head(shape):
    return lax.broadcasted_iota(jnp.int32, shape, len(shape) - 1) < HEAD_DIM


def lanes_of(p):
    return slice(p * LANES, (p + 1) * LANES)


def rows_of(p):
    return slice(p * HEAD_DIM, (p + 1) * HEAD_DIM)


def states_kernel(k_hbm, v_hbm, out_ref, k_ref, v_ref, arrived):
    copies = []
    for s in range(SLABS):
        lanes = slice(s * SLAB, (s + 1) * SLAB)
        copies.append([
            pltpu.make_async_copy(k_hbm.at[:, lanes], k_ref.at[:, lanes], arrived.at[0, s]),
            pltpu.make_async_copy(v_hbm.at[:, lanes], v_ref.at[:, lanes], arrived.at[1, s])])
        for copy in copies[-1]:
            copy.start()
    first = first_head((HEAD_DIM, LANES))
    share = out_ref.shape[1]
    for p in range(PAIRS):
        if p * LANES % SLAB == 0:
            for copy in copies[p * LANES // SLAB]:
                copy.wait()
        both = lax.dot_general(
            k_ref[:, lanes_of(p)], v_ref[:, lanes_of(p)], (((0,), (0,)), ((), ())),
            preferred_element_type=F32)
        packed = jnp.where(first, both[:HEAD_DIM], both[HEAD_DIM:])
        row = p * HEAD_DIM
        out_ref[row // share, row % share:row % share + HEAD_DIM, :] = packed.astype(out_ref.dtype)


def shares_kernel(chains, *refs):
    states, outs = refs[:chains], refs[chains:]
    me, chain = lax.axis_index("inner"), lax.axis_index("chain")
    for d, out in enumerate(outs):
        for e, state in enumerate(states):
            out[chain ^ e] = state[me ^ d]


def totals_kernel(*refs):
    *parts, out_ref, sent_ref = refs
    for c in range(out_ref.shape[0]):
        total = parts[0][c].astype(F32)
        for part in parts[1:]:
            total = total + part[c].astype(F32)
        out_ref[c] = total
        sent_ref[c] = total.astype(sent_ref.dtype)


def prefix_kernel(inner, planes, *refs):
    *ins, order = refs
    parts, totals, outs = ins[:inner], ins[inner:inner + planes], ins[inner + planes:]
    me, plane = lax.axis_index("inner"), lax.axis_index("outer")
    groups = jnp.zeros(order.shape[1:], F32)
    for c in range(outs[0].shape[0]):
        for d, part in zip(reversed(range(inner)), parts):
            order[me ^ d] = part[c].astype(F32)
        total = groups
        for e, there in zip(reversed(range(planes)), totals):
            there = there[c].astype(F32)
            groups = groups + there
            if e > 0:
                total = total + jnp.where((plane ^ e) < plane, there, 0.0)
        for i in range(inner):
            here = order[i]
            order[i] = total
            total = total + here
        for d, out in enumerate(outs):
            out[c] = order[me ^ d].astype(out.dtype)


def deal_kernel(inner, *refs):
    parts, outs = refs[:inner], refs[inner:]
    me, chain = lax.axis_index("inner"), lax.axis_index("chain")
    for d, part in zip(reversed(range(inner)), parts):
        for e, out in enumerate(outs):
            out[me ^ d] = part[chain ^ e]


def intra_kernel(q_ref, k_ref, v_ref, out_ref):
    rows = q_ref.shape[0]
    causal = (lax.broadcasted_iota(jnp.int32, (rows, rows), 0)
              >= lax.broadcasted_iota(jnp.int32, (rows, rows), 1))
    first = first_head((rows, LANES))
    zero = jnp.zeros((), BF16)
    for p in range(PAIRS):
        q, k, v = q_ref[:, lanes_of(p)], k_ref[:, lanes_of(p)], v_ref[:, lanes_of(p)]
        intra = []
        for mine in (first, ~first):
            scores = lax.dot_general(
                jnp.where(mine, q, zero), k, (((1,), (1,)), ((), ())),
                preferred_element_type=F32)
            scores = jnp.where(causal, scores, 0.0).astype(BF16)
            intra.append(jnp.dot(scores, v, preferred_element_type=F32))
        out_ref[:, lanes_of(p)] = jnp.where(first, intra[0], intra[1])


def attend_kernel(chains, q_ref, intra_ref, *refs):
    *dealt, out_hbm, out_ref, prefix_ref, sent = refs
    away = lax.axis_index("chain") ^ (chains - 1)
    for i in range(prefix_ref.shape[0]):
        prefix = dealt[0][i]
        for e in range(1, chains):
            prefix = jnp.where(away == e, dealt[e][i], prefix)
        prefix_ref[i] = prefix
    share = prefix_ref.shape[1]
    heads = SLAB // HEAD_DIM
    blocks = ([lax.broadcasted_iota(jnp.int32, (SLAB, SLAB), d) // HEAD_DIM for d in range(2)])
    same = blocks[0] == blocks[1]
    ones = jnp.where(same, 1.0, 0.0).astype(BF16)
    zero = jnp.zeros((), BF16)
    copies = []
    for s in range(HEADS // heads):
        lanes = slice(s * SLAB, (s + 1) * SLAB)
        rows = []
        for p in range(s * heads // 2, (s + 1) * heads // 2):
            row = p * HEAD_DIM
            pair = prefix_ref[row // share, row % share:row % share + HEAD_DIM, :]
            rows += [jnp.concatenate([pair] * (SLAB // LANES), axis=1)] * 2
        prefix = jnp.where(same, jnp.concatenate(rows, axis=0), zero)
        inter = jnp.dot(q_ref[:, lanes], prefix, preferred_element_type=F32)
        total = intra_ref[:, lanes] + inter
        square = total * total
        high = square.astype(BF16)
        low = (square - high.astype(F32)).astype(BF16)
        sums = (jnp.dot(high, ones, preferred_element_type=F32)
                + jnp.dot(low, ones, preferred_element_type=F32))
        out_ref[:, lanes] = (total * lax.rsqrt(sums * (1.0 / HEAD_DIM) + 1e-6)).astype(out_ref.dtype)
        copies.append(pltpu.make_async_copy(out_ref.at[:, lanes], out_hbm.at[:, lanes], sent.at[s]))
        copies[-1].start()
    for copy in copies:
        copy.wait()


def call(kernel, outs, *args, flops=0, scratch=(), source=pltpu.VMEM, result=pltpu.VMEM):
    moved = sum(a.size * a.dtype.itemsize for a in args)
    single = not isinstance(outs, list)
    outs = [outs] if single else outs
    got = pl.pallas_call(
        kernel,
        out_shape=[result(shape, dtype) for shape, dtype in outs],
        in_specs=[pl.BlockSpec(memory_space=source)] * len(args),
        out_specs=[pl.BlockSpec(memory_space=result)] * len(outs),
        scratch_shapes=scratch,
        cost_estimate=pl.CostEstimate(flops=flops, bytes_accessed=moved, transcendentals=0),
        compiler_params=pltpu.CompilerParams(vmem_limit_bytes=16 * 1024 * 1024),
    )(*[pltpu.with_memory_space_constraint(a, source) for a in args])
    return got[0] if single else got


def swapped(arrays, axis, chains):
    size = len(arrays)
    got = []
    for d in reversed(range(1, size)):
        pairs = [(i * chains + c, (i ^ d if c == chains - 1 else i) * chains + c) for i in range(size) for c in range(chains)]
        got.append(lax.ppermute(arrays[d], (axis, "chain"), pairs))
    return got + [arrays[0]]


def across(x, chains, e):
    return lax.ppermute(x, "chain", [(c, c ^ e) for c in range(chains)])


def per_device(chains, planes, inner, queries, keys, values):
    rows = queries.shape[0]
    share = (PAIRS * HEAD_DIM // inner, LANES)
    whole = ((inner,) + share, BF16)
    both = ((chains,) + share, BF16)
    states, keys, values = call(
        states_kernel, [whole, (keys.shape, keys.dtype), (values.shape, values.dtype)],
        keys, values, flops=2 * rows * LANES * LANES * PAIRS, source=pltpu.HBM,
        scratch=[pltpu.SemaphoreType.DMA((2, SLABS))])
    shares = call(functools.partial(shares_kernel, chains), [both] * inner,
                  states, *[across(states, chains, e) for e in range(1, chains)])
    mine = swapped(shares, "inner", chains)
    total, sent = call(totals_kernel, [(both[0], F32), both], *mine)
    totals = swapped([sent] * planes, "outer", chains)[:-1] + [total]
    before = call(functools.partial(prefix_kernel, inner, planes), [both] * inner, *mine, *totals,
                  scratch=[pltpu.VMEM((inner,) + share, F32)])
    *before, queries = lax.optimization_barrier((*before, queries))
    back = swapped(before, "inner", chains)
    dealt = call(functools.partial(deal_kernel, inner), [whole] * chains, *back)
    dealt = [dealt[0]] + [across(dealt[e], chains, e) for e in range(1, chains)]
    intra = call(intra_kernel, (queries.shape, F32), queries, keys, values,
                 flops=4 * rows * rows * HEADS * HEAD_DIM)
    return call(functools.partial(attend_kernel, chains), (queries.shape, BF16), queries, intra, *dealt,
                result=pltpu.HBM, flops=2 * rows * SLAB * HEADS * HEAD_DIM,
                scratch=[pltpu.VMEM(queries.shape, BF16), pltpu.VMEM(*whole),
                         pltpu.SemaphoreType.DMA((HEADS * HEAD_DIM // SLAB,))])


def solution(mesh):
    wide, chains = mesh.devices.shape
    inner = 4
    planes = wide // inner
    finer = jax.sharding.Mesh(mesh.devices.reshape(planes, inner, chains), ("outer", "inner", "chain"))
    spec = P(("chain", "outer", "inner"), None)
    return jax.shard_map(
        functools.partial(per_device, chains, planes, inner),
        mesh=finer,
        in_specs=(spec, spec, spec),
        out_specs=spec,
        check_vma=False,
    )
```

```python
import functools

import jax
import jax.numpy as jnp
from jax import lax
from jax.experimental import pallas as pl
from jax.experimental.pallas import tpu as pltpu
from jax.sharding import PartitionSpec as P

HEADS = 16
HEAD_DIM = 64
PAIRS = HEADS // 2
LANES = 2 * HEAD_DIM
SLABS = 4
SLAB = 256
VMEM = pl.BlockSpec(memory_space=pltpu.VMEM)
BF16 = jnp.bfloat16
F32 = jnp.float32


def first_head(shape):
    return lax.broadcasted_iota(jnp.int32, shape, len(shape) - 1) < HEAD_DIM


def lanes_of(p):
    return slice(p * LANES, (p + 1) * LANES)


def rows_of(p):
    return slice(p * HEAD_DIM, (p + 1) * HEAD_DIM)


def states_kernel(k_hbm, v_hbm, *refs):
    *outs, k_ref, v_ref, states, arrived = refs
    copies = []
    for s in range(SLABS):
        lanes = slice(s * SLAB, (s + 1) * SLAB)
        copies.append([
            pltpu.make_async_copy(k_hbm.at[:, lanes], k_ref.at[:, lanes], arrived.at[0, s]),
            pltpu.make_async_copy(v_hbm.at[:, lanes], v_ref.at[:, lanes], arrived.at[1, s])])
        for copy in copies[-1]:
            copy.start()
    first = first_head((HEAD_DIM, LANES))
    share = states.shape[1]
    for p in range(PAIRS):
        if p * LANES % SLAB == 0:
            for copy in copies[p * LANES // SLAB]:
                copy.wait()
        both = lax.dot_general(
            k_ref[:, lanes_of(p)], v_ref[:, lanes_of(p)], (((0,), (0,)), ((), ())),
            preferred_element_type=jnp.float32)
        packed = jnp.where(first, both[:HEAD_DIM], both[HEAD_DIM:])
        row = p * HEAD_DIM
        states[row // share, row % share:row % share + HEAD_DIM, :] = packed
    me = lax.axis_index("inner")
    for d, out in enumerate(outs):
        out[...] = states[me ^ d].astype(out.dtype)


def totals_kernel(*refs):
    *parts, own, out_ref, sent_ref = refs
    total = own[...]
    for part in parts:
        total = total + part[...].astype(F32)
    out_ref[...] = total
    sent_ref[...] = total.astype(sent_ref.dtype)


def planes_kernel(step, *refs):
    if step > 1:
        below_in, *refs = refs
    whole_in, there_ref, below_ref, whole_ref, *sent = refs
    there = there_ref[...].astype(F32)
    below = jnp.where((lax.axis_index("outer") & step) != 0, there, 0.0)
    below_ref[...] = below + below_in[...] if step > 1 else below
    whole = whole_in[...] + there
    whole_ref[...] = whole
    for ref in sent:
        ref[...] = whole.astype(ref.dtype)


def prefix_kernel(inner, *refs):
    *ins, order = refs
    parts, below, groups, outs = ins[:inner], ins[inner], ins[inner + 1:-inner], ins[-inner:]
    me, chain = lax.axis_index("inner"), lax.axis_index("chain")
    for d, part in zip(reversed(range(inner)), parts):
        order[me ^ d] = part[...].astype(F32)
    total = below[...]
    for d, group in enumerate(groups, 1):
        total = total + jnp.where((chain ^ d) < chain, group[...], 0.0)
    for i in range(inner):
        here = order[i]
        order[i] = total
        total = total + here
    for d, out in enumerate(outs):
        out[...] = order[me ^ d].astype(out.dtype)


def intra_kernel(q_ref, k_ref, v_ref, out_ref):
    rows = q_ref.shape[0]
    causal = (lax.broadcasted_iota(jnp.int32, (rows, rows), 0)
              >= lax.broadcasted_iota(jnp.int32, (rows, rows), 1))
    first = first_head((rows, LANES))
    zero = jnp.zeros((), BF16)
    for p in range(PAIRS):
        q, k, v = q_ref[:, lanes_of(p)], k_ref[:, lanes_of(p)], v_ref[:, lanes_of(p)]
        intra = []
        for mine in (first, ~first):
            scores = lax.dot_general(
                jnp.where(mine, q, zero), k, (((1,), (1,)), ((), ())),
                preferred_element_type=F32)
            scores = jnp.where(causal, scores, 0.0).astype(BF16)
            intra.append(jnp.dot(scores, v, preferred_element_type=F32))
        out_ref[:, lanes_of(p)] = jnp.where(first, intra[0], intra[1])


def attend_kernel(inner, q_ref, intra_ref, *refs):
    *parts, out_hbm, out_ref, prefix_ref, sent = refs
    me = lax.axis_index("inner")
    for d, part in zip(reversed(range(inner)), parts):
        prefix_ref[me ^ d] = part[...]
    share = prefix_ref.shape[1]
    heads = SLAB // HEAD_DIM
    blocks = ([lax.broadcasted_iota(jnp.int32, (SLAB, SLAB), d) // HEAD_DIM for d in range(2)])
    same = blocks[0] == blocks[1]
    ones = jnp.where(same, 1.0, 0.0).astype(BF16)
    zero = jnp.zeros((), BF16)
    copies = []
    for s in range(HEADS // heads):
        lanes = slice(s * SLAB, (s + 1) * SLAB)
        rows = []
        for p in range(s * heads // 2, (s + 1) * heads // 2):
            row = p * HEAD_DIM
            pair = prefix_ref[row // share, row % share:row % share + HEAD_DIM, :]
            rows += [jnp.concatenate([pair] * (SLAB // LANES), axis=1)] * 2
        prefix = jnp.where(same, jnp.concatenate(rows, axis=0), zero)
        inter = jnp.dot(q_ref[:, lanes], prefix, preferred_element_type=F32)
        total = intra_ref[:, lanes] + inter
        square = total * total
        sums = jnp.dot(square.astype(BF16), ones, preferred_element_type=F32)
        out_ref[:, lanes] = (total * lax.rsqrt(sums * (1.0 / HEAD_DIM) + 1e-6)).astype(out_ref.dtype)
        copies.append(pltpu.make_async_copy(out_ref.at[:, lanes], out_hbm.at[:, lanes], sent.at[s]))
        copies[-1].start()
    for copy in copies:
        copy.wait()


def call(kernel, outs, *args, flops=0, scratch=(), source=pltpu.VMEM, result=pltpu.VMEM):
    moved = sum(a.size * a.dtype.itemsize for a in args)
    single = not isinstance(outs, list)
    outs = [outs] if single else outs
    got = pl.pallas_call(
        kernel,
        out_shape=[result(shape, dtype) for shape, dtype in outs],
        in_specs=[pl.BlockSpec(memory_space=source)] * len(args),
        out_specs=[pl.BlockSpec(memory_space=result)] * len(outs),
        scratch_shapes=scratch,
        cost_estimate=pl.CostEstimate(flops=flops, bytes_accessed=moved, transcendentals=0),
        compiler_params=pltpu.CompilerParams(vmem_limit_bytes=16 * 1024 * 1024),
    )(*[pltpu.with_memory_space_constraint(a, source) for a in args])
    return got[0] if single else got


def swapped(arrays, axis, own):
    size = len(arrays)
    return [lax.ppermute(arrays[d], axis, [(i, i ^ d) for i in range(size)]) for d in reversed(range(1, size))] + [own]


def per_device(chains, planes, inner, queries, keys, values):
    rows = queries.shape[0]
    share = (PAIRS * HEAD_DIM // inner, LANES)
    own, *states, keys, values = call(
        states_kernel,
        [(share, F32)] + [(share, BF16)] * (inner - 1) + [(keys.shape, keys.dtype), (values.shape, values.dtype)],
        keys, values, flops=2 * rows * LANES * LANES * PAIRS, source=pltpu.HBM,
        scratch=[pltpu.VMEM((inner,) + share, F32), pltpu.SemaphoreType.DMA((2, SLABS))])
    mine = swapped([own] + states, "inner", own)
    total, sent = call(totals_kernel, [(share, F32), (share, BF16)], *mine)
    below, whole, step = [], total, 1
    while step < planes:
        there = lax.ppermute(sent, "outer", [(z, z ^ step) for z in range(planes)])
        last = 2 * step >= planes
        below, whole, *sent = call(
            functools.partial(planes_kernel, step), [(share, F32)] * 2 + [(share, BF16)] * (not last),
            *below, whole, there)
        below, sent, step = [below], sent[0] if sent else None, 2 * step
    groups = [lax.ppermute(whole, "chain", [(c, c ^ d) for c in range(chains)]) for d in range(1, chains)]
    before = call(functools.partial(prefix_kernel, inner), [(share, BF16)] * inner, *mine, *below, *groups,
                  scratch=[pltpu.VMEM((inner,) + share, F32)])
    prefix = swapped(before, "inner", before[0])
    intra = call(intra_kernel, (queries.shape, F32), queries, keys, values,
                 flops=4 * rows * rows * HEADS * HEAD_DIM)
    return call(functools.partial(attend_kernel, inner), (queries.shape, BF16), queries, intra, *prefix,
                result=pltpu.HBM, flops=2 * rows * SLAB * HEADS * HEAD_DIM,
                scratch=[pltpu.VMEM(queries.shape, BF16), pltpu.VMEM((inner,) + share, BF16),
                         pltpu.SemaphoreType.DMA((HEADS * HEAD_DIM // SLAB,))])


def solution(mesh):
    wide, chains = mesh.devices.shape
    inner = 4
    planes = wide // inner
    finer = jax.sharding.Mesh(mesh.devices.reshape(planes, inner, chains), ("outer", "inner", "chain"))
    spec = P(("chain", "outer", "inner"), None)
    return jax.shard_map(
        functools.partial(per_device, chains, planes, inner),
        mesh=finer,
        in_specs=(spec, spec, spec),
        out_specs=spec,
        check_vma=False,
    )
```

```python
import functools

import jax
import jax.numpy as jnp
from jax import lax
from jax.experimental import pallas as pl
from jax.experimental.pallas import tpu as pltpu
from jax.sharding import PartitionSpec as P

HEADS = 16
HEAD_DIM = 64
PAIRS = HEADS // 2
LANES = 2 * HEAD_DIM
SLABS = 4
HALVES = 2
SLAB = 256
VMEM = pl.BlockSpec(memory_space=pltpu.VMEM)
BF16 = jnp.bfloat16
F32 = jnp.float32


def first_head(shape):
    return lax.broadcasted_iota(jnp.int32, shape, len(shape) - 1) < HEAD_DIM


def lanes_of(p):
    return slice(p * LANES, (p + 1) * LANES)


def rows_of(p):
    return slice(p * HEAD_DIM, (p + 1) * HEAD_DIM)


def states_kernel(k_hbm, v_hbm, *refs):
    *outs, k_ref, v_ref, states, arrived = refs
    rows = k_ref.shape[0] // HALVES
    copies = []
    for s in range(SLABS):
        lanes = slice(s * SLAB, (s + 1) * SLAB)
        copies.append([])
        for r in range(HALVES):
            part = (pl.ds(r * rows, rows), lanes)
            copies[-1] += [
                pltpu.make_async_copy(k_hbm.at[part], k_ref.at[part], arrived.at[0, s, r]),
                pltpu.make_async_copy(v_hbm.at[part], v_ref.at[part], arrived.at[1, s, r])]
        for copy in copies[-1]:
            copy.start()
    first = first_head((HEAD_DIM, LANES))
    share = states.shape[1]
    for p in range(PAIRS):
        if p * LANES % SLAB == 0:
            for copy in copies[p * LANES // SLAB]:
                copy.wait()
        both = lax.dot_general(
            k_ref[:, lanes_of(p)], v_ref[:, lanes_of(p)], (((0,), (0,)), ((), ())),
            preferred_element_type=jnp.float32)
        packed = jnp.where(first, both[:HEAD_DIM], both[HEAD_DIM:])
        row = p * HEAD_DIM
        states[row // share, row % share:row % share + HEAD_DIM, :] = packed
    me = lax.axis_index("inner")
    for d, out in enumerate(outs):
        out[...] = states[me ^ d].astype(out.dtype)


def totals_kernel(*refs):
    *parts, own, out_ref, sent_ref = refs
    total = own[...]
    for part in parts:
        total = total + part[...].astype(F32)
    out_ref[...] = total
    sent_ref[...] = total.astype(sent_ref.dtype)


def planes_kernel(*refs):
    *totals, own, below_ref, whole_ref = refs
    plane = lax.axis_index("outer")
    whole = own[...]
    below = jnp.zeros_like(whole)
    for e, there in zip(reversed(range(1, len(totals) + 1)), totals):
        there = there[...].astype(F32)
        below = below + jnp.where((plane ^ e) < plane, there, 0.0)
        whole = whole + there
    below_ref[...] = below
    whole_ref[...] = whole


def prefix_kernel(inner, *refs):
    *ins, order = refs
    parts, below, groups, outs = ins[:inner], ins[inner], ins[inner + 1:-inner], ins[-inner:]
    me, chain = lax.axis_index("inner"), lax.axis_index("chain")
    for d, part in zip(reversed(range(inner)), parts):
        order[me ^ d] = part[...].astype(F32)
    total = below[...]
    for d, group in enumerate(groups, 1):
        total = total + jnp.where((chain ^ d) < chain, group[...], 0.0)
    for i in range(inner):
        here = order[i]
        order[i] = total
        total = total + here
    for d, out in enumerate(outs):
        out[...] = order[me ^ d].astype(out.dtype)


def intra_kernel(q_ref, k_ref, v_ref, out_ref):
    rows = q_ref.shape[0]
    causal = (lax.broadcasted_iota(jnp.int32, (rows, rows), 0)
              >= lax.broadcasted_iota(jnp.int32, (rows, rows), 1))
    first = first_head((rows, LANES))
    zero = jnp.zeros((), BF16)
    for p in range(PAIRS):
        q, k, v = q_ref[:, lanes_of(p)], k_ref[:, lanes_of(p)], v_ref[:, lanes_of(p)]
        intra = []
        for mine in (first, ~first):
            scores = lax.dot_general(
                jnp.where(mine, q, zero), k, (((1,), (1,)), ((), ())),
                preferred_element_type=F32)
            scores = jnp.where(causal, scores, 0.0).astype(BF16)
            intra.append(jnp.dot(scores, v, preferred_element_type=F32))
        out_ref[:, lanes_of(p)] = jnp.where(first, intra[0], intra[1])


def attend_kernel(inner, q_ref, intra_ref, *refs):
    *parts, out_hbm, out_ref, prefix_ref, sent = refs
    me = lax.axis_index("inner")
    for d, part in zip(reversed(range(inner)), parts):
        prefix_ref[me ^ d] = part[...]
    share = prefix_ref.shape[1]
    heads = SLAB // HEAD_DIM
    blocks = ([lax.broadcasted_iota(jnp.int32, (SLAB, SLAB), d) // HEAD_DIM for d in range(2)])
    same = blocks[0] == blocks[1]
    ones = jnp.where(same, 1.0, 0.0).astype(BF16)
    zero = jnp.zeros((), BF16)
    copies = []
    for s in range(HEADS // heads):
        lanes = slice(s * SLAB, (s + 1) * SLAB)
        rows = []
        for p in range(s * heads // 2, (s + 1) * heads // 2):
            row = p * HEAD_DIM
            pair = prefix_ref[row // share, row % share:row % share + HEAD_DIM, :]
            rows += [jnp.concatenate([pair] * (SLAB // LANES), axis=1)] * 2
        prefix = jnp.where(same, jnp.concatenate(rows, axis=0), zero)
        inter = jnp.dot(q_ref[:, lanes], prefix, preferred_element_type=F32)
        total = intra_ref[:, lanes] + inter
        square = total * total
        sums = jnp.dot(square.astype(BF16), ones, preferred_element_type=F32)
        out_ref[:, lanes] = (total * lax.rsqrt(sums * (1.0 / HEAD_DIM) + 1e-6)).astype(out_ref.dtype)
        copies.append(pltpu.make_async_copy(out_ref.at[:, lanes], out_hbm.at[:, lanes], sent.at[s]))
        copies[-1].start()
    for copy in copies:
        copy.wait()


def call(kernel, outs, *args, flops=0, scratch=(), source=pltpu.VMEM, result=pltpu.VMEM):
    moved = sum(a.size * a.dtype.itemsize for a in args)
    single = not isinstance(outs, list)
    outs = [outs] if single else outs
    got = pl.pallas_call(
        kernel,
        out_shape=[result(shape, dtype) for shape, dtype in outs],
        in_specs=[pl.BlockSpec(memory_space=source)] * len(args),
        out_specs=[pl.BlockSpec(memory_space=result)] * len(outs),
        scratch_shapes=scratch,
        cost_estimate=pl.CostEstimate(flops=flops, bytes_accessed=moved, transcendentals=0),
        compiler_params=pltpu.CompilerParams(vmem_limit_bytes=16 * 1024 * 1024),
    )(*[pltpu.with_memory_space_constraint(a, source) for a in args])
    return got[0] if single else got


def swapped(arrays, axis, own):
    size = len(arrays)
    return [lax.ppermute(arrays[d], axis, [(i, i ^ d) for i in range(size)]) for d in reversed(range(1, size))] + [own]


def per_device(chains, planes, inner, queries, keys, values):
    rows = queries.shape[0]
    share = (PAIRS * HEAD_DIM // inner, LANES)
    own, *states, keys, values = call(
        states_kernel,
        [(share, F32)] + [(share, BF16)] * (inner - 1) + [(keys.shape, keys.dtype), (values.shape, values.dtype)],
        keys, values, flops=2 * rows * LANES * LANES * PAIRS, source=pltpu.HBM,
        scratch=[pltpu.VMEM((inner,) + share, F32), pltpu.SemaphoreType.DMA((2, SLABS, HALVES))])
    mine = swapped([own] + states, "inner", own)
    total, sent = call(totals_kernel, [(share, F32), (share, BF16)], *mine)
    totals = swapped([sent] * planes, "outer", total)
    below, whole = call(planes_kernel, [(share, F32)] * 2, *totals)
    groups = [lax.ppermute(whole, "chain", [(c, c ^ d) for c in range(chains)]) for d in range(1, chains)]
    before = call(functools.partial(prefix_kernel, inner), [(share, BF16)] * inner, *mine, below, *groups,
                  scratch=[pltpu.VMEM((inner,) + share, F32)])
    prefix = swapped(before, "inner", before[0])
    intra = call(intra_kernel, (queries.shape, F32), queries, keys, values,
                 flops=4 * rows * rows * HEADS * HEAD_DIM)
    return call(functools.partial(attend_kernel, inner), (queries.shape, BF16), queries, intra, *prefix,
                result=pltpu.HBM, flops=2 * rows * SLAB * HEADS * HEAD_DIM,
                scratch=[pltpu.VMEM(queries.shape, BF16), pltpu.VMEM((inner,) + share, BF16),
                         pltpu.SemaphoreType.DMA((HEADS * HEAD_DIM // SLAB,))])


def solution(mesh):
    wide, chains = mesh.devices.shape
    inner = 4
    planes = wide // inner
    finer = jax.sharding.Mesh(mesh.devices.reshape(planes, inner, chains), ("outer", "inner", "chain"))
    spec = P(("chain", "outer", "inner"), None)
    return jax.shard_map(
        functools.partial(per_device, chains, planes, inner),
        mesh=finer,
        in_specs=(spec, spec, spec),
        out_specs=spec,
        check_vma=False,
    )
```

```python
import functools

import jax
import jax.numpy as jnp
from jax import lax
from jax.experimental import pallas as pl
from jax.experimental.pallas import tpu as pltpu
from jax.sharding import PartitionSpec as P

HEADS = 16
HEAD_DIM = 64
PAIRS = HEADS // 2
LANES = 2 * HEAD_DIM
SLABS = 4
HALVES = 2
SLAB = 256
VMEM = pl.BlockSpec(memory_space=pltpu.VMEM)
BF16 = jnp.bfloat16
F32 = jnp.float32


def first_head(shape):
    return lax.broadcasted_iota(jnp.int32, shape, len(shape) - 1) < HEAD_DIM


def lanes_of(p):
    return slice(p * LANES, (p + 1) * LANES)


def rows_of(p):
    return slice(p * HEAD_DIM, (p + 1) * HEAD_DIM)


def states_kernel(k_hbm, v_hbm, *refs):
    *outs, k_ref, v_ref, states, arrived = refs
    rows = k_ref.shape[0] // HALVES
    copies = []
    for s in range(SLABS):
        lanes = slice(s * SLAB, (s + 1) * SLAB)
        copies.append([])
        for r in range(HALVES):
            part = (pl.ds(r * rows, rows), lanes)
            copies[-1] += [
                pltpu.make_async_copy(k_hbm.at[part], k_ref.at[part], arrived.at[0, s, r]),
                pltpu.make_async_copy(v_hbm.at[part], v_ref.at[part], arrived.at[1, s, r])]
        for copy in copies[-1]:
            copy.start()
    first = first_head((HEAD_DIM, LANES))
    share = states.shape[1]
    for p in range(PAIRS):
        if p * LANES % SLAB == 0:
            for copy in copies[p * LANES // SLAB]:
                copy.wait()
        both = lax.dot_general(
            k_ref[:, lanes_of(p)], v_ref[:, lanes_of(p)], (((0,), (0,)), ((), ())),
            preferred_element_type=jnp.float32)
        packed = jnp.where(first, both[:HEAD_DIM], both[HEAD_DIM:])
        row = p * HEAD_DIM
        states[row // share, row % share:row % share + HEAD_DIM, :] = packed
    me = lax.axis_index("inner")
    for d, out in enumerate(outs):
        out[...] = states[me ^ d].astype(out.dtype)


def totals_kernel(*refs):
    *parts, own, out_ref, sent_ref = refs
    total = own[...]
    for part in parts:
        total = total + part[...].astype(F32)
    out_ref[...] = total
    sent_ref[...] = total.astype(sent_ref.dtype)


def planes_kernel(*refs):
    *totals, own, below_ref, whole_ref = refs
    plane = lax.axis_index("outer")
    whole = own[...]
    below = jnp.zeros_like(whole)
    for e, there in zip(reversed(range(1, len(totals) + 1)), totals):
        there = there[...].astype(F32)
        below = below + jnp.where((plane ^ e) < plane, there, 0.0)
        whole = whole + there
    below_ref[...] = below
    whole_ref[...] = whole


def prefix_kernel(inner, *refs):
    *ins, order = refs
    parts, below, groups, outs = ins[:inner], ins[inner], ins[inner + 1:-inner], ins[-inner:]
    me, chain = lax.axis_index("inner"), lax.axis_index("chain")
    for d, part in zip(reversed(range(inner)), parts):
        order[me ^ d] = part[...].astype(F32)
    total = below[...]
    for d, group in enumerate(groups, 1):
        total = total + jnp.where((chain ^ d) < chain, group[...], 0.0)
    for i in range(inner):
        here = order[i]
        order[i] = total
        total = total + here
    for d, out in enumerate(outs):
        out[...] = order[me ^ d].astype(out.dtype)


def intra_kernel(q_ref, k_ref, v_ref, out_ref):
    rows = q_ref.shape[0]
    causal = (lax.broadcasted_iota(jnp.int32, (rows, rows), 0)
              >= lax.broadcasted_iota(jnp.int32, (rows, rows), 1))
    first = first_head((rows, LANES))
    zero = jnp.zeros((), BF16)
    for p in range(PAIRS):
        q, k, v = q_ref[:, lanes_of(p)], k_ref[:, lanes_of(p)], v_ref[:, lanes_of(p)]
        intra = []
        for mine in (first, ~first):
            scores = lax.dot_general(
                jnp.where(mine, q, zero), k, (((1,), (1,)), ((), ())),
                preferred_element_type=F32)
            scores = jnp.where(causal, scores, 0.0).astype(BF16)
            intra.append(jnp.dot(scores, v, preferred_element_type=F32))
        out_ref[:, lanes_of(p)] = jnp.where(first, intra[0], intra[1])


def attend_kernel(inner, q_ref, intra_ref, *refs):
    *parts, out_hbm, out_ref, prefix_ref, sent = refs
    me = lax.axis_index("inner")
    for d, part in zip(reversed(range(inner)), parts):
        prefix_ref[me ^ d] = part[...]
    share = prefix_ref.shape[1]
    heads = SLAB // HEAD_DIM
    blocks = ([lax.broadcasted_iota(jnp.int32, (SLAB, SLAB), d) // HEAD_DIM for d in range(2)])
    same = blocks[0] == blocks[1]
    ones = jnp.where(same, 1.0, 0.0).astype(BF16)
    zero = jnp.zeros((), BF16)
    copies = []
    for s in range(HEADS // heads):
        lanes = slice(s * SLAB, (s + 1) * SLAB)
        rows = []
        for p in range(s * heads // 2, (s + 1) * heads // 2):
            row = p * HEAD_DIM
            pair = prefix_ref[row // share, row % share:row % share + HEAD_DIM, :]
            rows += [jnp.concatenate([pair] * (SLAB // LANES), axis=1)] * 2
        prefix = jnp.where(same, jnp.concatenate(rows, axis=0), zero)
        inter = jnp.dot(q_ref[:, lanes], prefix, preferred_element_type=F32)
        total = intra_ref[:, lanes] + inter
        square = total * total
        sums = jnp.dot(square.astype(BF16), ones, preferred_element_type=F32)
        out_ref[:, lanes] = (total * lax.rsqrt(sums * (1.0 / HEAD_DIM) + 1e-6)).astype(out_ref.dtype)
        copies.append(pltpu.make_async_copy(out_ref.at[:, lanes], out_hbm.at[:, lanes], sent.at[s]))
        copies[-1].start()
    for copy in copies:
        copy.wait()


def call(kernel, outs, *args, flops=0, scratch=(), source=pltpu.VMEM, result=pltpu.VMEM):
    moved = sum(a.size * a.dtype.itemsize for a in args)
    single = not isinstance(outs, list)
    outs = [outs] if single else outs
    got = pl.pallas_call(
        kernel,
        out_shape=[result(shape, dtype) for shape, dtype in outs],
        in_specs=[pl.BlockSpec(memory_space=source)] * len(args),
        out_specs=[pl.BlockSpec(memory_space=result)] * len(outs),
        scratch_shapes=scratch,
        cost_estimate=pl.CostEstimate(flops=flops, bytes_accessed=moved, transcendentals=0),
        compiler_params=pltpu.CompilerParams(vmem_limit_bytes=16 * 1024 * 1024),
    )(*[pltpu.with_memory_space_constraint(a, source) for a in args])
    return got[0] if single else got


def swapped(arrays, axis, own):
    size = len(arrays)
    return [lax.ppermute(arrays[d], axis, [(i, i ^ d) for i in range(size)]) for d in reversed(range(1, size))] + [own]


def per_device(chains, planes, inner, queries, keys, values):
    rows = queries.shape[0]
    share = (PAIRS * HEAD_DIM // inner, LANES)
    own, *states, keys, values = call(
        states_kernel,
        [(share, F32)] + [(share, BF16)] * (inner - 1) + [(keys.shape, keys.dtype), (values.shape, values.dtype)],
        keys, values, flops=2 * rows * LANES * LANES * PAIRS, source=pltpu.HBM,
        scratch=[pltpu.VMEM((inner,) + share, F32), pltpu.SemaphoreType.DMA((2, SLABS, HALVES))])
    mine = swapped([own] + states, "inner", own)
    total, sent = call(totals_kernel, [(share, F32), (share, BF16)], *mine)
    totals = swapped([sent] * planes, "outer", total)
    below, whole = call(planes_kernel, [(share, F32)] * 2, *totals)
    groups = [lax.ppermute(whole, "chain", [(c, c ^ d) for c in range(chains)]) for d in range(1, chains)]
    leads = lax.axis_index("chain") == 0

    def inside(queries, keys, values):
        return call(intra_kernel, (queries.shape, F32), queries, keys, values,
                    flops=4 * rows * rows * HEADS * HEAD_DIM)

    def way_back(*bases):
        before = call(functools.partial(prefix_kernel, inner), [(share, BF16)] * inner, *mine, *bases,
                      scratch=[pltpu.VMEM((inner,) + share, F32)])
        return swapped(before, "inner", before[0])

    prefix, intra = lax.cond(
        leads,
        lambda: (way_back(below), inside(queries, keys, values)),
        lambda: ([jnp.zeros(share, BF16)] * inner, inside(queries, keys, values)))
    prefix, groups = lax.optimization_barrier((prefix, groups))
    prefix = lax.cond(leads, lambda: prefix, lambda: way_back(below, *groups))
    return call(functools.partial(attend_kernel, inner), (queries.shape, BF16), queries, intra, *prefix,
                result=pltpu.HBM, flops=2 * rows * SLAB * HEADS * HEAD_DIM,
                scratch=[pltpu.VMEM(queries.shape, BF16), pltpu.VMEM((inner,) + share, BF16),
                         pltpu.SemaphoreType.DMA((HEADS * HEAD_DIM // SLAB,))])


def solution(mesh):
    wide, chains = mesh.devices.shape
    inner = 4
    planes = wide // inner
    finer = jax.sharding.Mesh(mesh.devices.reshape(planes, inner, chains), ("outer", "inner", "chain"))
    spec = P(("chain", "outer", "inner"), None)
    return jax.shard_map(
        functools.partial(per_device, chains, planes, inner),
        mesh=finer,
        in_specs=(spec, spec, spec),
        out_specs=spec,
        check_vma=False,
    )
```

```python
import functools

import jax
import jax.numpy as jnp
from jax import lax
from jax.experimental import pallas as pl
from jax.experimental.pallas import tpu as pltpu
from jax.sharding import PartitionSpec as P

HEADS = 16
HEAD_DIM = 64
PAIRS = HEADS // 2
LANES = 2 * HEAD_DIM
SLABS = 4
HALVES = 2
SLAB = 256
VMEM = pl.BlockSpec(memory_space=pltpu.VMEM)
BF16 = jnp.bfloat16
F32 = jnp.float32


def first_head(shape):
    return lax.broadcasted_iota(jnp.int32, shape, len(shape) - 1) < HEAD_DIM


def lanes_of(p):
    return slice(p * LANES, (p + 1) * LANES)


def rows_of(p):
    return slice(p * HEAD_DIM, (p + 1) * HEAD_DIM)


def states_kernel(k_hbm, v_hbm, *refs):
    *outs, k_ref, v_ref, states, arrived = refs
    rows = k_ref.shape[0] // HALVES
    copies = []
    for s in range(SLABS):
        lanes = slice(s * SLAB, (s + 1) * SLAB)
        copies.append([])
        for r in range(HALVES):
            part = (pl.ds(r * rows, rows), lanes)
            copies[-1] += [
                pltpu.make_async_copy(k_hbm.at[part], k_ref.at[part], arrived.at[0, s, r]),
                pltpu.make_async_copy(v_hbm.at[part], v_ref.at[part], arrived.at[1, s, r])]
        for copy in copies[-1]:
            copy.start()
    first = first_head((HEAD_DIM, LANES))
    share = states.shape[1]
    for p in range(PAIRS):
        if p * LANES % SLAB == 0:
            for copy in copies[p * LANES // SLAB]:
                copy.wait()
        both = lax.dot_general(
            k_ref[:, lanes_of(p)], v_ref[:, lanes_of(p)], (((0,), (0,)), ((), ())),
            preferred_element_type=jnp.float32)
        packed = jnp.where(first, both[:HEAD_DIM], both[HEAD_DIM:])
        row = p * HEAD_DIM
        states[row // share, row % share:row % share + HEAD_DIM, :] = packed
    me = lax.axis_index("inner")
    for d, out in enumerate(outs):
        out[...] = states[me ^ d].astype(out.dtype)


def totals_kernel(*refs):
    *parts, own, out_ref, sent_ref = refs
    total = own[...]
    for part in parts:
        total = total + part[...].astype(F32)
    out_ref[...] = total
    sent_ref[...] = total.astype(sent_ref.dtype)


def planes_kernel(*refs):
    *totals, own, below_ref, whole_ref = refs
    plane = lax.axis_index("outer")
    whole = own[...]
    below = jnp.zeros_like(whole)
    for e, there in enumerate(totals, 1):
        there = there[...].astype(F32)
        below = below + jnp.where((plane ^ e) < plane, there, 0.0)
        whole = whole + there
    below_ref[...] = below
    whole_ref[...] = whole


def prefix_kernel(inner, *refs):
    *ins, order = refs
    parts, below, groups, outs = ins[:inner], ins[inner], ins[inner + 1:-inner], ins[-inner:]
    me, chain = lax.axis_index("inner"), lax.axis_index("chain")
    for d, part in zip(reversed(range(inner)), parts):
        order[me ^ d] = part[...].astype(F32)
    total = below[...]
    for d, group in enumerate(groups, 1):
        total = total + jnp.where((chain ^ d) < chain, group[...], 0.0)
    for i in range(inner):
        here = order[i]
        order[i] = total
        total = total + here
    for d, out in enumerate(outs):
        out[...] = order[me ^ d].astype(out.dtype)


def intra_kernel(q_ref, k_ref, v_ref, out_ref):
    rows = q_ref.shape[0]
    causal = (lax.broadcasted_iota(jnp.int32, (rows, rows), 0)
              >= lax.broadcasted_iota(jnp.int32, (rows, rows), 1))
    first = first_head((rows, LANES))
    zero = jnp.zeros((), BF16)
    for p in range(PAIRS):
        q, k, v = q_ref[:, lanes_of(p)], k_ref[:, lanes_of(p)], v_ref[:, lanes_of(p)]
        intra = []
        for mine in (first, ~first):
            scores = lax.dot_general(
                jnp.where(mine, q, zero), k, (((1,), (1,)), ((), ())),
                preferred_element_type=F32)
            scores = jnp.where(causal, scores, 0.0).astype(BF16)
            intra.append(jnp.dot(scores, v, preferred_element_type=F32))
        out_ref[:, lanes_of(p)] = jnp.where(first, intra[0], intra[1])


def settle_kernel(inner, *refs):
    *parts, out_ref = refs
    me = lax.axis_index("inner")
    for d, part in zip(reversed(range(inner)), parts):
        out_ref[me ^ d] = part[...]


def unused_kernel(*refs):
    del refs


def attend_kernel(q_ref, first_intra, first_prefix, later_intra, later_prefix, *refs):
    leads = lax.axis_index("chain") == 0

    @pl.when(leads)
    def _():
        attend(q_ref, first_intra, first_prefix, *refs)

    @pl.when(~leads)
    def _():
        attend(q_ref, later_intra, later_prefix, *refs)


def attend(q_ref, intra_ref, prefix_ref, out_hbm, out_ref, sent):
    share = prefix_ref.shape[1]
    heads = SLAB // HEAD_DIM
    blocks = ([lax.broadcasted_iota(jnp.int32, (SLAB, SLAB), d) // HEAD_DIM for d in range(2)])
    same = blocks[0] == blocks[1]
    ones = jnp.where(same, 1.0, 0.0).astype(BF16)
    zero = jnp.zeros((), BF16)
    copies = []
    for s in range(HEADS // heads):
        lanes = slice(s * SLAB, (s + 1) * SLAB)
        rows = []
        for p in range(s * heads // 2, (s + 1) * heads // 2):
            row = p * HEAD_DIM
            pair = prefix_ref[row // share, row % share:row % share + HEAD_DIM, :]
            rows += [jnp.concatenate([pair] * (SLAB // LANES), axis=1)] * 2
        prefix = jnp.where(same, jnp.concatenate(rows, axis=0), zero)
        inter = jnp.dot(q_ref[:, lanes], prefix, preferred_element_type=F32)
        total = intra_ref[:, lanes] + inter
        square = total * total
        sums = jnp.dot(square.astype(BF16), ones, preferred_element_type=F32)
        out_ref[:, lanes] = (total * lax.rsqrt(sums * (1.0 / HEAD_DIM) + 1e-6)).astype(out_ref.dtype)
        copies.append(pltpu.make_async_copy(out_ref.at[:, lanes], out_hbm.at[:, lanes], sent.at[s]))
        copies[-1].start()
    for copy in copies:
        copy.wait()


def call(kernel, outs, *args, flops=0, scratch=(), source=pltpu.VMEM, result=pltpu.VMEM):
    moved = sum(a.size * a.dtype.itemsize for a in args)
    single = not isinstance(outs, list)
    outs = [outs] if single else outs
    got = pl.pallas_call(
        kernel,
        out_shape=[result(shape, dtype) for shape, dtype in outs],
        in_specs=[pl.BlockSpec(memory_space=source)] * len(args),
        out_specs=[pl.BlockSpec(memory_space=result)] * len(outs),
        scratch_shapes=scratch,
        cost_estimate=pl.CostEstimate(flops=flops, bytes_accessed=moved, transcendentals=0),
        compiler_params=pltpu.CompilerParams(vmem_limit_bytes=16 * 1024 * 1024),
    )(*[pltpu.with_memory_space_constraint(a, source) for a in args])
    return got[0] if single else got


def swapped(arrays, axis, own):
    size = len(arrays)
    return [lax.ppermute(arrays[d], axis, [(i, i ^ d) for i in range(size)]) for d in reversed(range(1, size))] + [own]


def per_device(chains, planes, inner, queries, keys, values):
    rows = queries.shape[0]
    share = (PAIRS * HEAD_DIM // inner, LANES)
    own, *states, keys, values = call(
        states_kernel,
        [(share, F32)] + [(share, BF16)] * (inner - 1) + [(keys.shape, keys.dtype), (values.shape, values.dtype)],
        keys, values, flops=2 * rows * LANES * LANES * PAIRS, source=pltpu.HBM,
        scratch=[pltpu.VMEM((inner,) + share, F32), pltpu.SemaphoreType.DMA((2, SLABS, HALVES))])
    mine = swapped([own] + states, "inner", own)
    total, sent = call(totals_kernel, [(share, F32), (share, BF16)], *mine)
    total, queries = lax.optimization_barrier((total, queries))
    *totals, _ = swapped([sent] * planes, "outer", total)
    totals = totals[::-1] + [total]
    below, whole = call(planes_kernel, [(share, F32)] * 2, *totals)
    groups = [lax.ppermute(whole, "chain", [(c, c ^ d) for c in range(chains)]) for d in range(1, chains)]
    leads = lax.axis_index("chain") == 0
    results = [(queries.shape, F32), ((inner,) + share, BF16)]

    def way_back(*bases):
        before = call(functools.partial(prefix_kernel, inner), [(share, BF16)] * inner, *mine, *bases,
                      scratch=[pltpu.VMEM((inner,) + share, F32)])
        prefix = swapped(before, "inner", before[0])
        intra = call(intra_kernel, results[0], queries, keys, values,
                     flops=4 * rows * rows * HEADS * HEAD_DIM)
        return intra, call(functools.partial(settle_kernel, inner), results[1], *prefix)

    def unused():
        return tuple(call(unused_kernel, results))

    first = lax.cond(leads, lambda: way_back(below), unused)
    first, groups = lax.optimization_barrier((first, groups))
    later = lax.cond(leads, unused, lambda: way_back(below, *groups))
    return call(attend_kernel, (queries.shape, BF16), queries, *first, *later,
                result=pltpu.HBM, flops=2 * rows * SLAB * HEADS * HEAD_DIM,
                scratch=[pltpu.VMEM(queries.shape, BF16), pltpu.SemaphoreType.DMA((HEADS * HEAD_DIM // SLAB,))])


def solution(mesh):
    wide, chains = mesh.devices.shape
    inner = 4
    planes = wide // inner
    finer = jax.sharding.Mesh(mesh.devices.reshape(planes, inner, chains), ("outer", "inner", "chain"))
    spec = P(("chain", "outer", "inner"), None)
    return jax.shard_map(
        functools.partial(per_device, chains, planes, inner),
        mesh=finer,
        in_specs=(spec, spec, spec),
        out_specs=spec,
        check_vma=False,
    )
```

```python
import functools

import jax
import jax.numpy as jnp
from jax import lax
from jax.experimental import pallas as pl
from jax.experimental.pallas import tpu as pltpu
from jax.sharding import PartitionSpec as P

HEADS = 16
HEAD_DIM = 64
PAIRS = HEADS // 2
LANES = 2 * HEAD_DIM
SLABS = 4
HALVES = 2
SLAB = 256
VMEM = pl.BlockSpec(memory_space=pltpu.VMEM)
BF16 = jnp.bfloat16
F32 = jnp.float32


def first_head(shape):
    return lax.broadcasted_iota(jnp.int32, shape, len(shape) - 1) < HEAD_DIM


def lanes_of(p):
    return slice(p * LANES, (p + 1) * LANES)


def rows_of(p):
    return slice(p * HEAD_DIM, (p + 1) * HEAD_DIM)


def states_kernel(k_hbm, v_hbm, *refs):
    *outs, k_ref, v_ref, states, arrived = refs
    rows = k_ref.shape[0] // HALVES
    copies = []
    for s in range(SLABS):
        lanes = slice(s * SLAB, (s + 1) * SLAB)
        copies.append([])
        for r in range(HALVES):
            part = (pl.ds(r * rows, rows), lanes)
            copies[-1] += [
                pltpu.make_async_copy(k_hbm.at[part], k_ref.at[part], arrived.at[0, s, r]),
                pltpu.make_async_copy(v_hbm.at[part], v_ref.at[part], arrived.at[1, s, r])]
        for copy in copies[-1]:
            copy.start()
    first = first_head((HEAD_DIM, LANES))
    share = states.shape[1]
    for p in range(PAIRS):
        if p * LANES % SLAB == 0:
            for copy in copies[p * LANES // SLAB]:
                copy.wait()
        both = lax.dot_general(
            k_ref[:, lanes_of(p)], v_ref[:, lanes_of(p)], (((0,), (0,)), ((), ())),
            preferred_element_type=jnp.float32)
        packed = jnp.where(first, both[:HEAD_DIM], both[HEAD_DIM:])
        row = p * HEAD_DIM
        states[row // share, row % share:row % share + HEAD_DIM, :] = packed
    me = lax.axis_index("inner")
    for d, out in enumerate(outs):
        out[...] = states[me ^ d].astype(out.dtype)


def totals_kernel(*refs):
    *parts, own, out_ref, sent_ref = refs
    total = own[...]
    for part in parts:
        total = total + part[...].astype(F32)
    out_ref[...] = total
    sent_ref[...] = total.astype(sent_ref.dtype)


def planes_kernel(*refs):
    *totals, own, below_ref, whole_ref = refs
    plane = lax.axis_index("outer")
    whole = own[...]
    below = jnp.zeros_like(whole)
    for e, there in enumerate(totals, 1):
        there = there[...].astype(F32)
        below = below + jnp.where((plane ^ e) < plane, there, 0.0)
        whole = whole + there
    below_ref[...] = below
    whole_ref[...] = whole


def prefix_kernel(inner, *refs):
    *ins, order = refs
    parts, below, groups, outs = ins[:inner], ins[inner], ins[inner + 1:-inner], ins[-inner:]
    me, chain = lax.axis_index("inner"), lax.axis_index("chain")
    for d, part in zip(reversed(range(inner)), parts):
        order[me ^ d] = part[...].astype(F32)
    total = below[...]
    for d, group in enumerate(groups, 1):
        total = total + jnp.where((chain ^ d) < chain, group[...], 0.0)
    for i in range(inner):
        here = order[i]
        order[i] = total
        total = total + here
    for d, out in enumerate(outs):
        out[...] = order[me ^ d].astype(out.dtype)


def intra_kernel(q_ref, k_ref, v_ref, out_ref):
    rows = q_ref.shape[0]
    causal = (lax.broadcasted_iota(jnp.int32, (rows, rows), 0)
              >= lax.broadcasted_iota(jnp.int32, (rows, rows), 1))
    first = first_head((rows, LANES))
    zero = jnp.zeros((), BF16)
    for p in range(PAIRS):
        q, k, v = q_ref[:, lanes_of(p)], k_ref[:, lanes_of(p)], v_ref[:, lanes_of(p)]
        intra = []
        for mine in (first, ~first):
            scores = lax.dot_general(
                jnp.where(mine, q, zero), k, (((1,), (1,)), ((), ())),
                preferred_element_type=F32)
            scores = jnp.where(causal, scores, 0.0).astype(BF16)
            intra.append(jnp.dot(scores, v, preferred_element_type=F32))
        out_ref[:, lanes_of(p)] = jnp.where(first, intra[0], intra[1])


def settle_kernel(inner, *refs):
    *parts, out_ref = refs
    me = lax.axis_index("inner")
    for d, part in zip(reversed(range(inner)), parts):
        out_ref[me ^ d] = part[...]


def unused_kernel(*refs):
    del refs


def attend_kernel(q_ref, intra_ref, prefix_ref, *refs):
    *_, out_hbm, out_ref, sent = refs
    share = prefix_ref.shape[1]
    heads = SLAB // HEAD_DIM
    blocks = ([lax.broadcasted_iota(jnp.int32, (SLAB, SLAB), d) // HEAD_DIM for d in range(2)])
    same = blocks[0] == blocks[1]
    ones = jnp.where(same, 1.0, 0.0).astype(BF16)
    zero = jnp.zeros((), BF16)
    copies = []
    for s in range(HEADS // heads):
        lanes = slice(s * SLAB, (s + 1) * SLAB)
        rows = []
        for p in range(s * heads // 2, (s + 1) * heads // 2):
            row = p * HEAD_DIM
            pair = prefix_ref[row // share, row % share:row % share + HEAD_DIM, :]
            rows += [jnp.concatenate([pair] * (SLAB // LANES), axis=1)] * 2
        prefix = jnp.where(same, jnp.concatenate(rows, axis=0), zero)
        inter = jnp.dot(q_ref[:, lanes], prefix, preferred_element_type=F32)
        total = intra_ref[:, lanes] + inter
        square = total * total
        sums = jnp.dot(square.astype(BF16), ones, preferred_element_type=F32)
        out_ref[:, lanes] = (total * lax.rsqrt(sums * (1.0 / HEAD_DIM) + 1e-6)).astype(out_ref.dtype)
        copies.append(pltpu.make_async_copy(out_ref.at[:, lanes], out_hbm.at[:, lanes], sent.at[s]))
        copies[-1].start()
    for copy in copies:
        copy.wait()


def call(kernel, outs, *args, flops=0, scratch=(), source=pltpu.VMEM, result=pltpu.VMEM, onto=None):
    moved = sum(a.size * a.dtype.itemsize for a in args)
    single = not isinstance(outs, list)
    outs = [outs] if single else outs
    specs = [pl.BlockSpec(memory_space=source)] * len(args)
    args = [pltpu.with_memory_space_constraint(a, source) for a in args]
    aliases = {}
    if onto is not None:
        aliases = {len(args): 0}
        specs.append(pl.BlockSpec(memory_space=result))
        args.append(pltpu.with_memory_space_constraint(onto, result))
    got = pl.pallas_call(
        kernel,
        out_shape=[result(shape, dtype) for shape, dtype in outs],
        in_specs=specs,
        out_specs=[pl.BlockSpec(memory_space=result)] * len(outs),
        scratch_shapes=scratch,
        input_output_aliases=aliases,
        cost_estimate=pl.CostEstimate(flops=flops, bytes_accessed=moved, transcendentals=0),
        compiler_params=pltpu.CompilerParams(vmem_limit_bytes=16 * 1024 * 1024),
    )(*args)
    return got[0] if single else got


def swapped(arrays, axis, own):
    size = len(arrays)
    return [lax.ppermute(arrays[d], axis, [(i, i ^ d) for i in range(size)]) for d in reversed(range(1, size))] + [own]


def per_device(chains, planes, inner, queries, keys, values):
    rows = queries.shape[0]
    share = (PAIRS * HEAD_DIM // inner, LANES)
    own, *states, keys, values = call(
        states_kernel,
        [(share, F32)] + [(share, BF16)] * (inner - 1) + [(keys.shape, keys.dtype), (values.shape, values.dtype)],
        keys, values, flops=2 * rows * LANES * LANES * PAIRS, source=pltpu.HBM,
        scratch=[pltpu.VMEM((inner,) + share, F32), pltpu.SemaphoreType.DMA((2, SLABS, HALVES))])
    mine = swapped([own] + states, "inner", own)
    total, sent = call(totals_kernel, [(share, F32), (share, BF16)], *mine)
    total, queries = lax.optimization_barrier((total, queries))
    *totals, _ = swapped([sent] * planes, "outer", total)
    totals = totals[::-1] + [total]
    below, whole = call(planes_kernel, [(share, F32)] * 2, *totals)
    groups = [lax.ppermute(whole, "chain", [(c, c ^ d) for c in range(chains)]) for d in range(1, chains)]
    leads = lax.axis_index("chain") == 0
    output = (queries.shape, BF16)

    def way_back(onto, *bases):
        before = call(functools.partial(prefix_kernel, inner), [(share, BF16)] * inner, *mine, *bases,
                      scratch=[pltpu.VMEM((inner,) + share, F32)])
        prefix = swapped(before, "inner", before[0])
        intra = call(intra_kernel, (queries.shape, F32), queries, keys, values,
                     flops=4 * rows * rows * HEADS * HEAD_DIM)
        prefix = call(functools.partial(settle_kernel, inner), ((inner,) + share, BF16), *prefix)
        return call(attend_kernel, output, queries, intra, prefix, result=pltpu.HBM, onto=onto,
                    flops=2 * rows * SLAB * HEADS * HEAD_DIM,
                    scratch=[pltpu.VMEM(*output), pltpu.SemaphoreType.DMA((HEADS * HEAD_DIM // SLAB,))])

    out = lax.cond(leads, lambda: way_back(None, below), lambda: call(unused_kernel, output, result=pltpu.HBM))
    out, groups = lax.optimization_barrier((out, groups))
    return lax.cond(leads, lambda out: out, lambda out: way_back(out, below, *groups), out)


def solution(mesh):
    wide, chains = mesh.devices.shape
    inner = 4
    planes = wide // inner
    finer = jax.sharding.Mesh(mesh.devices.reshape(planes, inner, chains), ("outer", "inner", "chain"))
    spec = P(("chain", "outer", "inner"), None)
    return jax.shard_map(
        functools.partial(per_device, chains, planes, inner),
        mesh=finer,
        in_specs=(spec, spec, spec),
        out_specs=spec,
        check_vma=False,
    )
```

```python
import functools

import jax
import jax.numpy as jnp
from jax import lax
from jax.experimental import pallas as pl
from jax.experimental.pallas import tpu as pltpu
from jax.sharding import PartitionSpec as P

HEADS = 16
HEAD_DIM = 64
PAIRS = HEADS // 2
LANES = 2 * HEAD_DIM
SLABS = 4
HALVES = 2
SLAB = 256
VMEM = pl.BlockSpec(memory_space=pltpu.VMEM)
BF16 = jnp.bfloat16
F32 = jnp.float32


def first_head(shape):
    return lax.broadcasted_iota(jnp.int32, shape, len(shape) - 1) < HEAD_DIM


def lanes_of(p):
    return slice(p * LANES, (p + 1) * LANES)


def rows_of(p):
    return slice(p * HEAD_DIM, (p + 1) * HEAD_DIM)


def states_kernel(k_hbm, v_hbm, *refs):
    *outs, k_ref, v_ref, states, arrived = refs
    rows = k_ref.shape[0] // HALVES
    copies = []
    for s in range(SLABS):
        lanes = slice(s * SLAB, (s + 1) * SLAB)
        copies.append([])
        for r in range(HALVES):
            part = (pl.ds(r * rows, rows), lanes)
            copies[-1] += [
                pltpu.make_async_copy(k_hbm.at[part], k_ref.at[part], arrived.at[0, s, r]),
                pltpu.make_async_copy(v_hbm.at[part], v_ref.at[part], arrived.at[1, s, r])]
        for copy in copies[-1]:
            copy.start()
    first = first_head((HEAD_DIM, LANES))
    share = states.shape[1]
    for p in range(PAIRS):
        if p * LANES % SLAB == 0:
            for copy in copies[p * LANES // SLAB]:
                copy.wait()
        both = lax.dot_general(
            k_ref[:, lanes_of(p)], v_ref[:, lanes_of(p)], (((0,), (0,)), ((), ())),
            preferred_element_type=jnp.float32)
        packed = jnp.where(first, both[:HEAD_DIM], both[HEAD_DIM:])
        row = p * HEAD_DIM
        states[row // share, row % share:row % share + HEAD_DIM, :] = packed
    me = lax.axis_index("inner")
    for d, out in enumerate(outs):
        out[...] = states[me ^ d].astype(out.dtype)


def totals_kernel(*refs):
    *parts, own, out_ref, sent_ref = refs
    total = own[...]
    for part in parts:
        total = total + part[...].astype(F32)
    out_ref[...] = total
    sent_ref[...] = total.astype(sent_ref.dtype)


def planes_kernel(*refs):
    *totals, own, below_ref, whole_ref = refs
    plane = lax.axis_index("outer")
    whole = own[...]
    below = jnp.zeros_like(whole)
    for e, there in enumerate(totals, 1):
        there = there[...].astype(F32)
        below = below + jnp.where((plane ^ e) < plane, there, 0.0)
        whole = whole + there
    below_ref[...] = below
    whole_ref[...] = whole


def prefix_kernel(inner, *refs):
    *ins, order = refs
    parts, below, groups, outs = ins[:inner], ins[inner], ins[inner + 1:-inner], ins[-inner:]
    me, chain = lax.axis_index("inner"), lax.axis_index("chain")
    for d, part in zip(reversed(range(inner)), parts):
        order[me ^ d] = part[...].astype(F32)
    total = below[...]
    for d, group in enumerate(groups, 1):
        total = total + jnp.where((chain ^ d) < chain, group[...], 0.0)
    for i in range(inner):
        here = order[i]
        order[i] = total
        total = total + here
    for d, out in enumerate(outs):
        out[...] = order[me ^ d].astype(out.dtype)


def intra_kernel(q_ref, k_ref, v_ref, out_ref):
    rows = q_ref.shape[0]
    causal = (lax.broadcasted_iota(jnp.int32, (rows, rows), 0)
              >= lax.broadcasted_iota(jnp.int32, (rows, rows), 1))
    first = first_head((rows, LANES))
    zero = jnp.zeros((), BF16)
    for p in range(PAIRS):
        q, k, v = q_ref[:, lanes_of(p)], k_ref[:, lanes_of(p)], v_ref[:, lanes_of(p)]
        intra = []
        for mine in (first, ~first):
            scores = lax.dot_general(
                jnp.where(mine, q, zero), k, (((1,), (1,)), ((), ())),
                preferred_element_type=F32)
            scores = jnp.where(causal, scores, 0.0).astype(BF16)
            intra.append(jnp.dot(scores, v, preferred_element_type=F32))
        out_ref[:, lanes_of(p)] = jnp.where(first, intra[0], intra[1])


def unused_kernel(*refs):
    del refs


def attend_kernel(away, q_ref, intra_ref, *refs):
    parts, (out_hbm, out_ref, sent) = refs[:len(away)], refs[-3:]
    blocks = ([lax.broadcasted_iota(jnp.int32, (SLAB, SLAB), d) // HEAD_DIM for d in range(2)])
    same = blocks[0] == blocks[1]
    ones = jnp.where(same, 1.0, 0.0).astype(BF16)
    zero = jnp.zeros((), BF16)
    me = lax.axis_index("inner")
    width = parts[0].shape[0] // HEAD_DIM * LANES
    copies = []
    for j, (d, part) in enumerate(zip(away, parts)):
        for t in range(width // SLAB):
            lanes = pl.ds(pl.multiple_of((me ^ d) * width + t * SLAB, SLAB), SLAB)
            rows = []
            for p in range(t * SLAB // LANES, (t + 1) * SLAB // LANES):
                rows += [jnp.concatenate([part[rows_of(p), :]] * (SLAB // LANES), axis=1)] * 2
            prefix = jnp.where(same, jnp.concatenate(rows, axis=0), zero)
            inter = jnp.dot(q_ref[:, lanes], prefix, preferred_element_type=F32)
            total = intra_ref[:, lanes] + inter
            square = total * total
            sums = jnp.dot(square.astype(BF16), ones, preferred_element_type=F32)
            n = len(copies)
            out_ref[n] = (total * lax.rsqrt(sums * (1.0 / HEAD_DIM) + 1e-6)).astype(out_ref.dtype)
            copies.append(pltpu.make_async_copy(out_ref.at[n], out_hbm.at[:, lanes], sent.at[n]))
            copies[-1].start()
    for copy in copies:
        copy.wait()


def call(kernel, outs, *args, flops=0, scratch=(), source=pltpu.VMEM, result=pltpu.VMEM, onto=None):
    moved = sum(a.size * a.dtype.itemsize for a in args)
    single = not isinstance(outs, list)
    outs = [outs] if single else outs
    specs = [pl.BlockSpec(memory_space=source)] * len(args)
    args = [pltpu.with_memory_space_constraint(a, source) for a in args]
    aliases = {}
    if onto is not None:
        aliases = {len(args): 0}
        specs.append(pl.BlockSpec(memory_space=result))
        args.append(pltpu.with_memory_space_constraint(onto, result))
    got = pl.pallas_call(
        kernel,
        out_shape=[result(shape, dtype) for shape, dtype in outs],
        in_specs=specs,
        out_specs=[pl.BlockSpec(memory_space=result)] * len(outs),
        scratch_shapes=scratch,
        input_output_aliases=aliases,
        cost_estimate=pl.CostEstimate(flops=flops, bytes_accessed=moved, transcendentals=0),
        compiler_params=pltpu.CompilerParams(vmem_limit_bytes=16 * 1024 * 1024),
    )(*args)
    return got[0] if single else got


def swapped(arrays, axis, own):
    size = len(arrays)
    return [lax.ppermute(arrays[d], axis, [(i, i ^ d) for i in range(size)]) for d in reversed(range(1, size))] + [own]


def per_device(chains, planes, inner, queries, keys, values):
    rows = queries.shape[0]
    share = (PAIRS * HEAD_DIM // inner, LANES)
    own, *states, keys, values = call(
        states_kernel,
        [(share, F32)] + [(share, BF16)] * (inner - 1) + [(keys.shape, keys.dtype), (values.shape, values.dtype)],
        keys, values, flops=2 * rows * LANES * LANES * PAIRS, source=pltpu.HBM,
        scratch=[pltpu.VMEM((inner,) + share, F32), pltpu.SemaphoreType.DMA((2, SLABS, HALVES))])
    mine = swapped([own] + states, "inner", own)
    total, sent = call(totals_kernel, [(share, F32), (share, BF16)], *mine)
    total, queries = lax.optimization_barrier((total, queries))
    *totals, _ = swapped([sent] * planes, "outer", total)
    totals = totals[::-1] + [total]
    below, whole = call(planes_kernel, [(share, F32)] * 2, *totals)
    groups = [lax.ppermute(whole, "chain", [(c, c ^ d) for c in range(chains)]) for d in range(1, chains)]
    leads = lax.axis_index("chain") == 0
    output = (queries.shape, BF16)

    def way_back(onto, *bases):
        before = call(functools.partial(prefix_kernel, inner), [(share, BF16)] * inner, *mine, *bases,
                      scratch=[pltpu.VMEM((inner,) + share, F32)])
        prefix = swapped(before, "inner", before[0])
        intra = call(intra_kernel, (queries.shape, F32), queries, keys, values,
                     flops=4 * rows * rows * HEADS * HEAD_DIM)
        for away in (0, inner - 1), tuple(range(1, inner - 1)):
            slabs = len(away) * HEADS * HEAD_DIM // inner // SLAB
            onto = call(functools.partial(attend_kernel, away), output, queries, intra,
                        *[prefix[inner - 1 - d] for d in away], result=pltpu.HBM, onto=onto,
                        flops=2 * rows * SLAB * slabs * SLAB,
                        scratch=[pltpu.VMEM((slabs, rows, SLAB), BF16), pltpu.SemaphoreType.DMA((slabs,))])
        return onto

    out = lax.cond(leads, lambda: way_back(None, below), lambda: call(unused_kernel, output, result=pltpu.HBM))
    out, groups = lax.optimization_barrier((out, groups))
    return lax.cond(leads, lambda out: out, lambda out: way_back(out, below, *groups), out)


def solution(mesh):
    wide, chains = mesh.devices.shape
    inner = 4
    planes = wide // inner
    finer = jax.sharding.Mesh(mesh.devices.reshape(planes, inner, chains), ("outer", "inner", "chain"))
    spec = P(("chain", "outer", "inner"), None)
    return jax.shard_map(
        functools.partial(per_device, chains, planes, inner),
        mesh=finer,
        in_specs=(spec, spec, spec),
        out_specs=spec,
        check_vma=False,
    )
```

```python
import functools

import jax
import jax.numpy as jnp
from jax import lax
from jax.experimental import pallas as pl
from jax.experimental.pallas import tpu as pltpu
from jax.sharding import PartitionSpec as P

HEADS = 16
HEAD_DIM = 64
PAIRS = HEADS // 2
LANES = 2 * HEAD_DIM
SLABS = 4
HALVES = 2
SLAB = 256
VMEM = pl.BlockSpec(memory_space=pltpu.VMEM)
BF16 = jnp.bfloat16
F32 = jnp.float32


def first_head(shape):
    return lax.broadcasted_iota(jnp.int32, shape, len(shape) - 1) < HEAD_DIM


def lanes_of(p):
    return slice(p * LANES, (p + 1) * LANES)


def rows_of(p):
    return slice(p * HEAD_DIM, (p + 1) * HEAD_DIM)


def states_kernel(k_hbm, v_hbm, *refs):
    *outs, k_ref, v_ref, states, arrived = refs
    rows = k_ref.shape[0] // HALVES
    copies = []
    for s in range(SLABS):
        lanes = slice(s * SLAB, (s + 1) * SLAB)
        copies.append([])
        for r in range(HALVES):
            part = (pl.ds(r * rows, rows), lanes)
            copies[-1] += [
                pltpu.make_async_copy(k_hbm.at[part], k_ref.at[part], arrived.at[0, s, r]),
                pltpu.make_async_copy(v_hbm.at[part], v_ref.at[part], arrived.at[1, s, r])]
        for copy in copies[-1]:
            copy.start()
    first = first_head((HEAD_DIM, LANES))
    share = states.shape[1]
    for p in range(PAIRS):
        if p * LANES % SLAB == 0:
            for copy in copies[p * LANES // SLAB]:
                copy.wait()
        both = lax.dot_general(
            k_ref[:, lanes_of(p)], v_ref[:, lanes_of(p)], (((0,), (0,)), ((), ())),
            preferred_element_type=jnp.float32)
        packed = jnp.where(first, both[:HEAD_DIM], both[HEAD_DIM:])
        row = p * HEAD_DIM
        states[row // share, row % share:row % share + HEAD_DIM, :] = packed
    me = lax.axis_index("inner")
    for d, out in enumerate(outs):
        out[...] = states[me ^ d].astype(out.dtype)


def totals_kernel(*refs):
    *parts, own, out_ref, sent_ref = refs
    total = own[...]
    for part in parts:
        total = total + part[...].astype(F32)
    out_ref[...] = total
    sent_ref[...] = total.astype(sent_ref.dtype)


def planes_kernel(*refs):
    *totals, own, below_ref, whole_ref = refs
    plane = lax.axis_index("outer")
    whole = own[...]
    below = jnp.zeros_like(whole)
    for s, there in zip(reversed(range(1, len(totals) + 1)), totals):
        there = there[...].astype(F32)
        below = below + jnp.where(plane >= s, there, 0.0)
        whole = whole + there
    below_ref[...] = below
    whole_ref[...] = whole


def prefix_kernel(inner, *refs):
    *ins, order = refs
    parts, below, groups, outs = ins[:inner], ins[inner], ins[inner + 1:-inner], ins[-inner:]
    me, chain = lax.axis_index("inner"), lax.axis_index("chain")
    for d, part in zip(reversed(range(inner)), parts):
        order[me ^ d] = part[...].astype(F32)
    total = below[...]
    for d, group in enumerate(groups, 1):
        total = total + jnp.where((chain ^ d) < chain, group[...], 0.0)
    for i in range(inner):
        here = order[i]
        order[i] = total
        total = total + here
    for d, out in enumerate(outs):
        out[...] = order[me ^ d].astype(out.dtype)


def intra_kernel(q_ref, k_ref, v_ref, out_ref):
    rows = q_ref.shape[0]
    causal = (lax.broadcasted_iota(jnp.int32, (rows, rows), 0)
              >= lax.broadcasted_iota(jnp.int32, (rows, rows), 1))
    first = first_head((rows, LANES))
    zero = jnp.zeros((), BF16)
    for p in range(PAIRS):
        q, k, v = q_ref[:, lanes_of(p)], k_ref[:, lanes_of(p)], v_ref[:, lanes_of(p)]
        intra = []
        for mine in (first, ~first):
            scores = lax.dot_general(
                jnp.where(mine, q, zero), k, (((1,), (1,)), ((), ())),
                preferred_element_type=F32)
            scores = jnp.where(causal, scores, 0.0).astype(BF16)
            intra.append(jnp.dot(scores, v, preferred_element_type=F32))
        out_ref[:, lanes_of(p)] = jnp.where(first, intra[0], intra[1])


def settle_kernel(inner, *refs):
    *parts, out_ref = refs
    me = lax.axis_index("inner")
    for d, part in zip(reversed(range(inner)), parts):
        out_ref[me ^ d] = part[...]


def unused_kernel(*refs):
    del refs


def attend_kernel(q_ref, intra_ref, prefix_ref, *refs):
    *_, out_hbm, out_ref, sent = refs
    share = prefix_ref.shape[1]
    heads = SLAB // HEAD_DIM
    blocks = ([lax.broadcasted_iota(jnp.int32, (SLAB, SLAB), d) // HEAD_DIM for d in range(2)])
    same = blocks[0] == blocks[1]
    ones = jnp.where(same, 1.0, 0.0).astype(BF16)
    zero = jnp.zeros((), BF16)
    copies = []
    for s in range(HEADS // heads):
        lanes = slice(s * SLAB, (s + 1) * SLAB)
        rows = []
        for p in range(s * heads // 2, (s + 1) * heads // 2):
            row = p * HEAD_DIM
            pair = prefix_ref[row // share, row % share:row % share + HEAD_DIM, :]
            rows += [jnp.concatenate([pair] * (SLAB // LANES), axis=1)] * 2
        prefix = jnp.where(same, jnp.concatenate(rows, axis=0), zero)
        inter = jnp.dot(q_ref[:, lanes], prefix, preferred_element_type=F32)
        total = intra_ref[:, lanes] + inter
        square = total * total
        sums = jnp.dot(square.astype(BF16), ones, preferred_element_type=F32)
        out_ref[:, lanes] = (total * lax.rsqrt(sums * (1.0 / HEAD_DIM) + 1e-6)).astype(out_ref.dtype)
        copies.append(pltpu.make_async_copy(out_ref.at[:, lanes], out_hbm.at[:, lanes], sent.at[s]))
        copies[-1].start()
    for copy in copies:
        copy.wait()


def call(kernel, outs, *args, flops=0, scratch=(), source=pltpu.VMEM, result=pltpu.VMEM, onto=None):
    moved = sum(a.size * a.dtype.itemsize for a in args)
    single = not isinstance(outs, list)
    outs = [outs] if single else outs
    specs = [pl.BlockSpec(memory_space=source)] * len(args)
    args = [pltpu.with_memory_space_constraint(a, source) for a in args]
    aliases = {}
    if onto is not None:
        aliases = {len(args): 0}
        specs.append(pl.BlockSpec(memory_space=result))
        args.append(pltpu.with_memory_space_constraint(onto, result))
    got = pl.pallas_call(
        kernel,
        out_shape=[result(shape, dtype) for shape, dtype in outs],
        in_specs=specs,
        out_specs=[pl.BlockSpec(memory_space=result)] * len(outs),
        scratch_shapes=scratch,
        input_output_aliases=aliases,
        cost_estimate=pl.CostEstimate(flops=flops, bytes_accessed=moved, transcendentals=0),
        compiler_params=pltpu.CompilerParams(vmem_limit_bytes=16 * 1024 * 1024),
    )(*args)
    return got[0] if single else got


def swapped(arrays, axis, own):
    size = len(arrays)
    return [lax.ppermute(arrays[d], axis, [(i, i ^ d) for i in range(size)]) for d in reversed(range(1, size))] + [own]


def per_device(chains, planes, inner, queries, keys, values):
    rows = queries.shape[0]
    share = (PAIRS * HEAD_DIM // inner, LANES)
    own, *states, keys, values = call(
        states_kernel,
        [(share, F32)] + [(share, BF16)] * (inner - 1) + [(keys.shape, keys.dtype), (values.shape, values.dtype)],
        keys, values, flops=2 * rows * LANES * LANES * PAIRS, source=pltpu.HBM,
        scratch=[pltpu.VMEM((inner,) + share, F32), pltpu.SemaphoreType.DMA((2, SLABS, HALVES))])
    mine = swapped([own] + states, "inner", own)
    total, sent = call(totals_kernel, [(share, F32), (share, BF16)], *mine)
    total, queries = lax.optimization_barrier((total, queries))
    totals = [lax.ppermute(sent, "outer", [(z, (z + s) % planes) for z in range(planes)])
              for s in reversed(range(1, planes))] + [total]
    below, whole = call(planes_kernel, [(share, F32)] * 2, *totals)
    groups = [lax.ppermute(whole, "chain", [(c, c ^ d) for c in range(chains)]) for d in range(1, chains)]
    leads = lax.axis_index("chain") == 0
    output = (queries.shape, BF16)

    def way_back(onto, *bases):
        before = call(functools.partial(prefix_kernel, inner), [(share, BF16)] * inner, *mine, *bases,
                      scratch=[pltpu.VMEM((inner,) + share, F32)])
        prefix = swapped(before, "inner", before[0])
        intra = call(intra_kernel, (queries.shape, F32), queries, keys, values,
                     flops=4 * rows * rows * HEADS * HEAD_DIM)
        prefix = call(functools.partial(settle_kernel, inner), ((inner,) + share, BF16), *prefix)
        return call(attend_kernel, output, queries, intra, prefix, result=pltpu.HBM, onto=onto,
                    flops=2 * rows * SLAB * HEADS * HEAD_DIM,
                    scratch=[pltpu.VMEM(*output), pltpu.SemaphoreType.DMA((HEADS * HEAD_DIM // SLAB,))])

    out = lax.cond(leads, lambda: way_back(None, below), lambda: call(unused_kernel, output, result=pltpu.HBM))
    out, groups = lax.optimization_barrier((out, groups))
    return lax.cond(leads, lambda out: out, lambda out: way_back(out, below, *groups), out)


def solution(mesh):
    wide, chains = mesh.devices.shape
    inner = 4
    planes = wide // inner
    finer = jax.sharding.Mesh(mesh.devices.reshape(planes, inner, chains), ("outer", "inner", "chain"))
    spec = P(("chain", "outer", "inner"), None)
    return jax.shard_map(
        functools.partial(per_device, chains, planes, inner),
        mesh=finer,
        in_specs=(spec, spec, spec),
        out_specs=spec,
        check_vma=False,
    )
```

```python
import functools

import jax
import jax.numpy as jnp
from jax import lax
from jax.experimental import pallas as pl
from jax.experimental.pallas import tpu as pltpu
from jax.sharding import PartitionSpec as P

HEADS = 16
HEAD_DIM = 64
PAIRS = HEADS // 2
LANES = 2 * HEAD_DIM
SLABS = 4
SLAB = 256
VMEM = pl.BlockSpec(memory_space=pltpu.VMEM)
BF16 = jnp.bfloat16
F32 = jnp.float32


def first_head(shape):
    return lax.broadcasted_iota(jnp.int32, shape, len(shape) - 1) < HEAD_DIM


def lanes_of(p):
    return slice(p * LANES, (p + 1) * LANES)


def rows_of(p):
    return slice(p * HEAD_DIM, (p + 1) * HEAD_DIM)


def share_states(k_ref, v_ref, out_ref, away):
    first = first_head((HEAD_DIM, LANES))
    width = out_ref.shape[0] // HEAD_DIM * LANES
    start = (lax.axis_index("inner") ^ away) * width
    for p in range(width // LANES):
        lanes = pl.ds(pl.multiple_of(start + p * LANES, LANES), LANES)
        both = lax.dot_general(
            k_ref[:, lanes], v_ref[:, lanes], (((0,), (0,)), ((), ())), preferred_element_type=F32)
        out_ref[rows_of(p), :] = jnp.where(first, both[:HEAD_DIM], both[HEAD_DIM:]).astype(out_ref.dtype)


def first_kernel(away, k_hbm, v_hbm, out_ref, k_ref, v_ref, arrived):
    copies = []
    for s in range(SLABS):
        lanes = slice(s * SLAB, (s + 1) * SLAB)
        copies += [
            pltpu.make_async_copy(k_hbm.at[:, lanes], k_ref.at[:, lanes], arrived.at[0, s]),
            pltpu.make_async_copy(v_hbm.at[:, lanes], v_ref.at[:, lanes], arrived.at[1, s])]
    for copy in copies:
        copy.start()
    for copy in copies:
        copy.wait()
    share_states(k_ref, v_ref, out_ref, away)


def near_kernel(away, k_ref, v_ref, out_ref):
    share_states(k_ref, v_ref, out_ref, away)


def own_kernel(k_ref, v_ref, q_hbm, out_ref, q_ref, arrived):
    copy = pltpu.make_async_copy(q_hbm, q_ref, arrived)
    copy.start()
    share_states(k_ref, v_ref, out_ref, 0)
    copy.wait()


def totals_kernel(*refs):
    *parts, own, out_ref, sent_ref = refs
    total = own[...]
    for part in parts:
        total = total + part[...].astype(F32)
    out_ref[...] = total
    sent_ref[...] = total.astype(sent_ref.dtype)


def planes_kernel(*refs):
    *totals, own, below_ref, whole_ref = refs
    plane = lax.axis_index("outer")
    whole = own[...]
    below = jnp.zeros_like(whole)
    for s, there in zip(reversed(range(1, len(totals) + 1)), totals):
        there = there[...].astype(F32)
        below = below + jnp.where(plane >= s, there, 0.0)
        whole = whole + there
    below_ref[...] = below
    whole_ref[...] = whole


def prefix_kernel(inner, *refs):
    *ins, order = refs
    parts, below, groups, outs = ins[:inner], ins[inner], ins[inner + 1:-inner], ins[-inner:]
    me, chain = lax.axis_index("inner"), lax.axis_index("chain")
    for d, part in zip(reversed(range(inner)), parts):
        order[me ^ d] = part[...].astype(F32)
    total = below[...]
    for d, group in enumerate(groups, 1):
        total = total + jnp.where((chain ^ d) < chain, group[...], 0.0)
    for i in range(inner):
        here = order[i]
        order[i] = total
        total = total + here
    for d, out in enumerate(outs):
        out[...] = order[me ^ d].astype(out.dtype)


def intra_kernel(q_ref, k_ref, v_ref, out_ref):
    rows = q_ref.shape[0]
    causal = (lax.broadcasted_iota(jnp.int32, (rows, rows), 0)
              >= lax.broadcasted_iota(jnp.int32, (rows, rows), 1))
    first = first_head((rows, LANES))
    zero = jnp.zeros((), BF16)
    for p in range(PAIRS):
        q, k, v = q_ref[:, lanes_of(p)], k_ref[:, lanes_of(p)], v_ref[:, lanes_of(p)]
        intra = []
        for mine in (first, ~first):
            scores = lax.dot_general(
                jnp.where(mine, q, zero), k, (((1,), (1,)), ((), ())),
                preferred_element_type=F32)
            scores = jnp.where(causal, scores, 0.0).astype(BF16)
            intra.append(jnp.dot(scores, v, preferred_element_type=F32))
        out_ref[:, lanes_of(p)] = jnp.where(first, intra[0], intra[1])


def settle_kernel(inner, *refs):
    *parts, out_ref = refs
    me = lax.axis_index("inner")
    for d, part in zip(reversed(range(inner)), parts):
        out_ref[me ^ d] = part[...]


def unused_kernel(*refs):
    del refs


def attend_kernel(q_ref, intra_ref, prefix_ref, *refs):
    *_, out_hbm, out_ref, sent = refs
    share = prefix_ref.shape[1]
    heads = SLAB // HEAD_DIM
    blocks = ([lax.broadcasted_iota(jnp.int32, (SLAB, SLAB), d) // HEAD_DIM for d in range(2)])
    same = blocks[0] == blocks[1]
    ones = jnp.where(same, 1.0, 0.0).astype(BF16)
    zero = jnp.zeros((), BF16)
    copies = []
    for s in range(HEADS // heads):
        lanes = slice(s * SLAB, (s + 1) * SLAB)
        rows = []
        for p in range(s * heads // 2, (s + 1) * heads // 2):
            row = p * HEAD_DIM
            pair = prefix_ref[row // share, row % share:row % share + HEAD_DIM, :]
            rows += [jnp.concatenate([pair] * (SLAB // LANES), axis=1)] * 2
        prefix = jnp.where(same, jnp.concatenate(rows, axis=0), zero)
        inter = jnp.dot(q_ref[:, lanes], prefix, preferred_element_type=F32)
        total = intra_ref[:, lanes] + inter
        square = total * total
        sums = jnp.dot(square.astype(BF16), ones, preferred_element_type=F32)
        out_ref[:, lanes] = (total * lax.rsqrt(sums * (1.0 / HEAD_DIM) + 1e-6)).astype(out_ref.dtype)
        copies.append(pltpu.make_async_copy(out_ref.at[:, lanes], out_hbm.at[:, lanes], sent.at[s]))
        copies[-1].start()
    for copy in copies:
        copy.wait()


def call(kernel, outs, *args, flops=0, scratch=(), source=pltpu.VMEM, result=pltpu.VMEM, onto=None):
    moved = sum(a.size * a.dtype.itemsize for a in args)
    single = not isinstance(outs, list)
    outs = [outs] if single else outs
    sources = source if isinstance(source, list) else [source] * len(args)
    specs = [pl.BlockSpec(memory_space=s) for s in sources]
    args = [pltpu.with_memory_space_constraint(a, s) for a, s in zip(args, sources)]
    aliases = {}
    if onto is not None:
        aliases = {len(args): 0}
        specs.append(pl.BlockSpec(memory_space=result))
        args.append(pltpu.with_memory_space_constraint(onto, result))
    got = pl.pallas_call(
        kernel,
        out_shape=[result(shape, dtype) for shape, dtype in outs],
        in_specs=specs,
        out_specs=[pl.BlockSpec(memory_space=result)] * len(outs),
        scratch_shapes=scratch,
        input_output_aliases=aliases,
        cost_estimate=pl.CostEstimate(flops=flops, bytes_accessed=moved, transcendentals=0),
        compiler_params=pltpu.CompilerParams(vmem_limit_bytes=16 * 1024 * 1024),
    )(*args)
    return got[0] if single else got


def swapped(arrays, axis, own):
    size = len(arrays)
    return [lax.ppermute(arrays[d], axis, [(i, i ^ d) for i in range(size)]) for d in reversed(range(1, size))] + [own]


def per_device(chains, planes, inner, queries, keys, values):
    rows = queries.shape[0]
    share = (PAIRS * HEAD_DIM // inner, LANES)
    flops = 2 * rows * LANES * share[0] // HEAD_DIM * LANES
    sent, keys, values = call(
        functools.partial(first_kernel, 1),
        [(share, BF16), (keys.shape, keys.dtype), (values.shape, values.dtype)], keys, values,
        flops=flops, source=pltpu.HBM, scratch=[pltpu.SemaphoreType.DMA((2, SLABS))])
    near = [call(functools.partial(near_kernel, d), (share, BF16), keys, values, flops=flops) for d in range(2, inner)]
    own, queries = call(
        own_kernel, [(share, F32), (queries.shape, queries.dtype)], keys, values, queries, flops=flops,
        source=[pltpu.VMEM, pltpu.VMEM, pltpu.HBM], scratch=[pltpu.SemaphoreType.DMA(())])
    mine = swapped([own, sent] + near, "inner", own)
    total, sent = call(totals_kernel, [(share, F32), (share, BF16)], *mine)
    totals = [lax.ppermute(sent, "outer", [(z, (z + s) % planes) for z in range(planes)])
              for s in reversed(range(1, planes))] + [total]
    below, whole = call(planes_kernel, [(share, F32)] * 2, *totals)
    groups = [lax.ppermute(whole, "chain", [(c, c ^ d) for c in range(chains)]) for d in range(1, chains)]
    leads = lax.axis_index("chain") == 0
    output = (queries.shape, BF16)

    def way_back(onto, *bases):
        before = call(functools.partial(prefix_kernel, inner), [(share, BF16)] * inner, *mine, *bases,
                      scratch=[pltpu.VMEM((inner,) + share, F32)])
        prefix = swapped(before, "inner", before[0])
        intra = call(intra_kernel, (queries.shape, F32), queries, keys, values,
                     flops=4 * rows * rows * HEADS * HEAD_DIM)
        prefix = call(functools.partial(settle_kernel, inner), ((inner,) + share, BF16), *prefix)
        return call(attend_kernel, output, queries, intra, prefix, result=pltpu.HBM, onto=onto,
                    flops=2 * rows * SLAB * HEADS * HEAD_DIM,
                    scratch=[pltpu.VMEM(*output), pltpu.SemaphoreType.DMA((HEADS * HEAD_DIM // SLAB,))])

    out = lax.cond(leads, lambda: way_back(None, below), lambda: call(unused_kernel, output, result=pltpu.HBM))
    out, groups = lax.optimization_barrier((out, groups))
    return lax.cond(leads, lambda out: out, lambda out: way_back(out, below, *groups), out)


def solution(mesh):
    wide, chains = mesh.devices.shape
    inner = 4
    planes = wide // inner
    finer = jax.sharding.Mesh(mesh.devices.reshape(planes, inner, chains), ("outer", "inner", "chain"))
    spec = P(("chain", "outer", "inner"), None)
    return jax.shard_map(
        functools.partial(per_device, chains, planes, inner),
        mesh=finer,
        in_specs=(spec, spec, spec),
        out_specs=spec,
        check_vma=False,
    )
```

```python
import functools

import jax
import jax.numpy as jnp
from jax import lax
from jax.experimental import pallas as pl
from jax.experimental.pallas import tpu as pltpu
from jax.sharding import PartitionSpec as P

HEADS = 16
HEAD_DIM = 64
PAIRS = HEADS // 2
LANES = 2 * HEAD_DIM
SLABS = 4
HALVES = 2
SLAB = 256
VMEM = pl.BlockSpec(memory_space=pltpu.VMEM)
BF16 = jnp.bfloat16
F32 = jnp.float32


def first_head(shape):
    return lax.broadcasted_iota(jnp.int32, shape, len(shape) - 1) < HEAD_DIM


def lanes_of(p):
    return slice(p * LANES, (p + 1) * LANES)


def rows_of(p):
    return slice(p * HEAD_DIM, (p + 1) * HEAD_DIM)


def states_kernel(k_hbm, v_hbm, *refs):
    *outs, k_ref, v_ref, states, arrived = refs
    rows = k_ref.shape[0] // HALVES
    copies = []
    for s in range(SLABS):
        lanes = slice(s * SLAB, (s + 1) * SLAB)
        copies.append([])
        for r in range(HALVES):
            part = (pl.ds(r * rows, rows), lanes)
            copies[-1] += [
                pltpu.make_async_copy(k_hbm.at[part], k_ref.at[part], arrived.at[0, s, r]),
                pltpu.make_async_copy(v_hbm.at[part], v_ref.at[part], arrived.at[1, s, r])]
        for copy in copies[-1]:
            copy.start()
    first = first_head((HEAD_DIM, LANES))
    share = states.shape[1]
    for slab in copies:
        for copy in slab:
            copy.wait()
    for p in range(PAIRS):
        both = lax.dot_general(
            k_ref[:, lanes_of(p)], v_ref[:, lanes_of(p)], (((0,), (0,)), ((), ())),
            preferred_element_type=jnp.float32)
        packed = jnp.where(first, both[:HEAD_DIM], both[HEAD_DIM:])
        row = p * HEAD_DIM
        states[row // share, row % share:row % share + HEAD_DIM, :] = packed
    me = lax.axis_index("inner")
    for d, out in enumerate(outs):
        out[...] = states[me ^ d].astype(out.dtype)


def load_kernel(q_hbm, after_ref, q_ref, arrived):
    del after_ref
    copy = pltpu.make_async_copy(q_hbm, q_ref, arrived)
    copy.start()
    copy.wait()


def totals_kernel(*refs):
    _, *parts, own, out_ref, sent_ref = refs
    total = own[...]
    for part in parts:
        total = total + part[...].astype(F32)
    out_ref[...] = total
    sent_ref[...] = total.astype(sent_ref.dtype)


def planes_kernel(*refs):
    *totals, own, below_ref, whole_ref = refs
    plane = lax.axis_index("outer")
    whole = own[...]
    below = jnp.zeros_like(whole)
    for s, there in zip(reversed(range(1, len(totals) + 1)), totals):
        there = there[...].astype(F32)
        below = below + jnp.where(plane >= s, there, 0.0)
        whole = whole + there
    below_ref[...] = below
    whole_ref[...] = whole


def prefix_kernel(inner, *refs):
    *ins, order = refs
    parts, below, groups, outs = ins[:inner], ins[inner], ins[inner + 1:-inner], ins[-inner:]
    me, chain = lax.axis_index("inner"), lax.axis_index("chain")
    for d, part in zip(reversed(range(inner)), parts):
        order[me ^ d] = part[...].astype(F32)
    total = below[...]
    for d, group in enumerate(groups, 1):
        total = total + jnp.where((chain ^ d) < chain, group[...], 0.0)
    for i in range(inner):
        here = order[i]
        order[i] = total
        total = total + here
    for d, out in enumerate(outs):
        out[...] = order[me ^ d].astype(out.dtype)


def intra_kernel(q_ref, k_ref, v_ref, out_ref):
    rows = q_ref.shape[0]
    causal = (lax.broadcasted_iota(jnp.int32, (rows, rows), 0)
              >= lax.broadcasted_iota(jnp.int32, (rows, rows), 1))
    first = first_head((rows, LANES))
    zero = jnp.zeros((), BF16)
    for p in range(PAIRS):
        q, k, v = q_ref[:, lanes_of(p)], k_ref[:, lanes_of(p)], v_ref[:, lanes_of(p)]
        intra = []
        for mine in (first, ~first):
            scores = lax.dot_general(
                jnp.where(mine, q, zero), k, (((1,), (1,)), ((), ())),
                preferred_element_type=F32)
            scores = jnp.where(causal, scores, 0.0).astype(BF16)
            intra.append(jnp.dot(scores, v, preferred_element_type=F32))
        out_ref[:, lanes_of(p)] = jnp.where(first, intra[0], intra[1])


def settle_kernel(inner, *refs):
    *parts, out_ref = refs
    me = lax.axis_index("inner")
    for d, part in zip(reversed(range(inner)), parts):
        out_ref[me ^ d] = part[...]


def unused_kernel(*refs):
    del refs


def attend_kernel(q_ref, intra_ref, prefix_ref, *refs):
    *_, out_hbm, out_ref, sent = refs
    share = prefix_ref.shape[1]
    heads = SLAB // HEAD_DIM
    blocks = ([lax.broadcasted_iota(jnp.int32, (SLAB, SLAB), d) // HEAD_DIM for d in range(2)])
    same = blocks[0] == blocks[1]
    ones = jnp.where(same, 1.0, 0.0).astype(BF16)
    zero = jnp.zeros((), BF16)
    copies = []
    for s in range(HEADS // heads):
        lanes = slice(s * SLAB, (s + 1) * SLAB)
        rows = []
        for p in range(s * heads // 2, (s + 1) * heads // 2):
            row = p * HEAD_DIM
            pair = prefix_ref[row // share, row % share:row % share + HEAD_DIM, :]
            rows += [jnp.concatenate([pair] * (SLAB // LANES), axis=1)] * 2
        prefix = jnp.where(same, jnp.concatenate(rows, axis=0), zero)
        inter = jnp.dot(q_ref[:, lanes], prefix, preferred_element_type=F32)
        total = intra_ref[:, lanes] + inter
        square = total * total
        sums = jnp.dot(square.astype(BF16), ones, preferred_element_type=F32)
        out_ref[:, lanes] = (total * lax.rsqrt(sums * (1.0 / HEAD_DIM) + 1e-6)).astype(out_ref.dtype)
        copies.append(pltpu.make_async_copy(out_ref.at[:, lanes], out_hbm.at[:, lanes], sent.at[s]))
        copies[-1].start()
    for copy in copies:
        copy.wait()


def call(kernel, outs, *args, flops=0, scratch=(), source=pltpu.VMEM, result=pltpu.VMEM, onto=None):
    moved = sum(a.size * a.dtype.itemsize for a in args)
    single = not isinstance(outs, list)
    outs = [outs] if single else outs
    sources = source if isinstance(source, list) else [source] * len(args)
    specs = [pl.BlockSpec(memory_space=s) for s in sources]
    args = [pltpu.with_memory_space_constraint(a, s) for a, s in zip(args, sources)]
    aliases = {}
    if onto is not None:
        aliases = {len(args): 0}
        specs.append(pl.BlockSpec(memory_space=result))
        args.append(pltpu.with_memory_space_constraint(onto, result))
    got = pl.pallas_call(
        kernel,
        out_shape=[result(shape, dtype) for shape, dtype in outs],
        in_specs=specs,
        out_specs=[pl.BlockSpec(memory_space=result)] * len(outs),
        scratch_shapes=scratch,
        input_output_aliases=aliases,
        cost_estimate=pl.CostEstimate(flops=flops, bytes_accessed=moved, transcendentals=0),
        compiler_params=pltpu.CompilerParams(vmem_limit_bytes=16 * 1024 * 1024),
    )(*args)
    return got[0] if single else got


def swapped(arrays, axis, own):
    size = len(arrays)
    return [lax.ppermute(arrays[d], axis, [(i, i ^ d) for i in range(size)]) for d in reversed(range(1, size))] + [own]


def per_device(chains, planes, inner, queries, keys, values):
    rows = queries.shape[0]
    share = (PAIRS * HEAD_DIM // inner, LANES)
    own, *states, keys, values = call(
        states_kernel,
        [(share, F32)] + [(share, BF16)] * (inner - 1) + [(keys.shape, keys.dtype), (values.shape, values.dtype)],
        keys, values, flops=2 * rows * LANES * LANES * PAIRS, source=pltpu.HBM,
        scratch=[pltpu.VMEM((inner,) + share, F32), pltpu.SemaphoreType.DMA((2, SLABS, HALVES))])
    queries = call(load_kernel, (queries.shape, queries.dtype), queries, own,
                   source=[pltpu.HBM, pltpu.VMEM], scratch=[pltpu.SemaphoreType.DMA(())])
    mine = swapped([own] + states, "inner", own)
    total, sent = call(totals_kernel, [(share, F32), (share, BF16)], queries, *mine)
    totals = [lax.ppermute(sent, "outer", [(z, (z + s) % planes) for z in range(planes)])
              for s in reversed(range(1, planes))] + [total]
    below, whole = call(planes_kernel, [(share, F32)] * 2, *totals)
    groups = [lax.ppermute(whole, "chain", [(c, c ^ d) for c in range(chains)]) for d in range(1, chains)]
    leads = lax.axis_index("chain") == 0
    output = (queries.shape, BF16)

    def way_back(onto, *bases):
        before = call(functools.partial(prefix_kernel, inner), [(share, BF16)] * inner, *mine, *bases,
                      scratch=[pltpu.VMEM((inner,) + share, F32)])
        prefix = swapped(before, "inner", before[0])
        intra = call(intra_kernel, (queries.shape, F32), queries, keys, values,
                     flops=4 * rows * rows * HEADS * HEAD_DIM)
        prefix = call(functools.partial(settle_kernel, inner), ((inner,) + share, BF16), *prefix)
        return call(attend_kernel, output, queries, intra, prefix, result=pltpu.HBM, onto=onto,
                    flops=2 * rows * SLAB * HEADS * HEAD_DIM,
                    scratch=[pltpu.VMEM(*output), pltpu.SemaphoreType.DMA((HEADS * HEAD_DIM // SLAB,))])

    out = lax.cond(leads, lambda: way_back(None, below), lambda: call(unused_kernel, output, result=pltpu.HBM))
    out, groups = lax.optimization_barrier((out, groups))
    return lax.cond(leads, lambda out: out, lambda out: way_back(out, below, *groups), out)


def solution(mesh):
    wide, chains = mesh.devices.shape
    inner = 4
    planes = wide // inner
    finer = jax.sharding.Mesh(mesh.devices.reshape(planes, inner, chains), ("outer", "inner", "chain"))
    spec = P(("chain", "outer", "inner"), None)
    return jax.shard_map(
        functools.partial(per_device, chains, planes, inner),
        mesh=finer,
        in_specs=(spec, spec, spec),
        out_specs=spec,
        check_vma=False,
    )
```

```python
import functools

import jax
import jax.numpy as jnp
from jax import lax
from jax.experimental import pallas as pl
from jax.experimental.pallas import tpu as pltpu
from jax.sharding import PartitionSpec as P

HEADS = 16
HEAD_DIM = 64
PAIRS = HEADS // 2
LANES = 2 * HEAD_DIM
HALVES = 2
SLAB = 256
VMEM = pl.BlockSpec(memory_space=pltpu.VMEM)
BF16 = jnp.bfloat16
F32 = jnp.float32


def first_head(shape):
    return lax.broadcasted_iota(jnp.int32, shape, len(shape) - 1) < HEAD_DIM


def lanes_of(p):
    return slice(p * LANES, (p + 1) * LANES)


def rows_of(p):
    return slice(p * HEAD_DIM, (p + 1) * HEAD_DIM)


def states_kernel(k_hbm, v_hbm, *refs):
    *outs, k_ref, v_ref, states, arrived = refs
    rows = k_ref.shape[0] // HALVES
    copies = []
    for r in range(HALVES):
        part = pl.ds(r * rows, rows)
        copies.append([
            pltpu.make_async_copy(k_hbm.at[part], k_ref.at[part], arrived.at[0, r]),
            pltpu.make_async_copy(v_hbm.at[part], v_ref.at[part], arrived.at[1, r])])
        for copy in copies[-1]:
            copy.start()
    first = first_head((HEAD_DIM, LANES))
    share = states.shape[1]
    for half in copies:
        for copy in half:
            copy.wait()
    for p in range(PAIRS):
        both = lax.dot_general(
            k_ref[:, lanes_of(p)], v_ref[:, lanes_of(p)], (((0,), (0,)), ((), ())),
            preferred_element_type=jnp.float32)
        packed = jnp.where(first, both[:HEAD_DIM], both[HEAD_DIM:])
        row = p * HEAD_DIM
        states[row // share, row % share:row % share + HEAD_DIM, :] = packed
    me = lax.axis_index("inner")
    for d, out in enumerate(outs):
        out[...] = states[me ^ d].astype(out.dtype)


def load_kernel(q_hbm, after_ref, q_ref, arrived):
    del after_ref
    copy = pltpu.make_async_copy(q_hbm, q_ref, arrived)
    copy.start()
    copy.wait()


def totals_kernel(*refs):
    _, *parts, own, out_ref, sent_ref = refs
    total = own[...]
    for part in parts:
        total = total + part[...].astype(F32)
    out_ref[...] = total
    sent_ref[...] = total.astype(sent_ref.dtype)


def planes_kernel(*refs):
    *totals, own, below_ref, whole_ref = refs
    plane = lax.axis_index("outer")
    whole = own[...]
    below = jnp.zeros_like(whole)
    for s, there in zip(reversed(range(1, len(totals) + 1)), totals):
        there = there[...].astype(F32)
        below = below + jnp.where(plane >= s, there, 0.0)
        whole = whole + there
    below_ref[...] = below
    whole_ref[...] = whole


def prefix_kernel(inner, *refs):
    *ins, order = refs
    parts, below, groups, outs = ins[:inner], ins[inner], ins[inner + 1:-inner], ins[-inner:]
    me, chain = lax.axis_index("inner"), lax.axis_index("chain")
    for d, part in zip(reversed(range(inner)), parts):
        order[me ^ d] = part[...].astype(F32)
    total = below[...]
    for d, group in enumerate(groups, 1):
        total = total + jnp.where((chain ^ d) < chain, group[...], 0.0)
    for i in range(inner):
        here = order[i]
        order[i] = total
        total = total + here
    for d, out in enumerate(outs):
        out[...] = order[me ^ d].astype(out.dtype)


def intra_kernel(q_ref, k_ref, v_ref, out_ref):
    rows = q_ref.shape[0]
    causal = (lax.broadcasted_iota(jnp.int32, (rows, rows), 0)
              >= lax.broadcasted_iota(jnp.int32, (rows, rows), 1))
    first = first_head((rows, LANES))
    zero = jnp.zeros((), BF16)
    for p in range(PAIRS):
        q, k, v = q_ref[:, lanes_of(p)], k_ref[:, lanes_of(p)], v_ref[:, lanes_of(p)]
        intra = []
        for mine in (first, ~first):
            scores = lax.dot_general(
                jnp.where(mine, q, zero), k, (((1,), (1,)), ((), ())),
                preferred_element_type=F32)
            scores = jnp.where(causal, scores, 0.0).astype(BF16)
            intra.append(jnp.dot(scores, v, preferred_element_type=F32))
        out_ref[:, lanes_of(p)] = jnp.where(first, intra[0], intra[1])


def settle_kernel(inner, *refs):
    *parts, out_ref = refs
    me = lax.axis_index("inner")
    for d, part in zip(reversed(range(inner)), parts):
        out_ref[me ^ d] = part[...]


def unused_kernel(*refs):
    del refs


def attend_kernel(q_ref, intra_ref, prefix_ref, *refs):
    *_, out_hbm, out_ref, sent = refs
    share = prefix_ref.shape[1]
    heads = SLAB // HEAD_DIM
    blocks = ([lax.broadcasted_iota(jnp.int32, (SLAB, SLAB), d) // HEAD_DIM for d in range(2)])
    same = blocks[0] == blocks[1]
    ones = jnp.where(same, 1.0, 0.0).astype(BF16)
    zero = jnp.zeros((), BF16)
    copies = []
    for s in range(HEADS // heads):
        lanes = slice(s * SLAB, (s + 1) * SLAB)
        rows = []
        for p in range(s * heads // 2, (s + 1) * heads // 2):
            row = p * HEAD_DIM
            pair = prefix_ref[row // share, row % share:row % share + HEAD_DIM, :]
            rows += [jnp.concatenate([pair] * (SLAB // LANES), axis=1)] * 2
        prefix = jnp.where(same, jnp.concatenate(rows, axis=0), zero)
        inter = jnp.dot(q_ref[:, lanes], prefix, preferred_element_type=F32)
        total = intra_ref[:, lanes] + inter
        square = total * total
        sums = jnp.dot(square.astype(BF16), ones, preferred_element_type=F32)
        out_ref[:, lanes] = (total * lax.rsqrt(sums * (1.0 / HEAD_DIM) + 1e-6)).astype(out_ref.dtype)
        copies.append(pltpu.make_async_copy(out_ref.at[:, lanes], out_hbm.at[:, lanes], sent.at[s]))
        copies[-1].start()
    for copy in copies:
        copy.wait()


def call(kernel, outs, *args, flops=0, scratch=(), source=pltpu.VMEM, result=pltpu.VMEM, onto=None):
    moved = sum(a.size * a.dtype.itemsize for a in args)
    single = not isinstance(outs, list)
    outs = [outs] if single else outs
    sources = source if isinstance(source, list) else [source] * len(args)
    specs = [pl.BlockSpec(memory_space=s) for s in sources]
    args = [pltpu.with_memory_space_constraint(a, s) for a, s in zip(args, sources)]
    aliases = {}
    if onto is not None:
        aliases = {len(args): 0}
        specs.append(pl.BlockSpec(memory_space=result))
        args.append(pltpu.with_memory_space_constraint(onto, result))
    got = pl.pallas_call(
        kernel,
        out_shape=[result(shape, dtype) for shape, dtype in outs],
        in_specs=specs,
        out_specs=[pl.BlockSpec(memory_space=result)] * len(outs),
        scratch_shapes=scratch,
        input_output_aliases=aliases,
        cost_estimate=pl.CostEstimate(flops=flops, bytes_accessed=moved, transcendentals=0),
        compiler_params=pltpu.CompilerParams(vmem_limit_bytes=16 * 1024 * 1024),
    )(*args)
    return got[0] if single else got


def swapped(arrays, axis, own):
    size = len(arrays)
    return [lax.ppermute(arrays[d], axis, [(i, i ^ d) for i in range(size)]) for d in reversed(range(1, size))] + [own]


def per_device(chains, planes, inner, queries, keys, values):
    rows = queries.shape[0]
    share = (PAIRS * HEAD_DIM // inner, LANES)
    own, *states, keys, values = call(
        states_kernel,
        [(share, F32)] + [(share, BF16)] * (inner - 1) + [(keys.shape, keys.dtype), (values.shape, values.dtype)],
        keys, values, flops=2 * rows * LANES * LANES * PAIRS, source=pltpu.HBM,
        scratch=[pltpu.VMEM((inner,) + share, F32), pltpu.SemaphoreType.DMA((2, HALVES))])
    queries = call(load_kernel, (queries.shape, queries.dtype), queries, own,
                   source=[pltpu.HBM, pltpu.VMEM], scratch=[pltpu.SemaphoreType.DMA(())])
    mine = swapped([own] + states, "inner", own)
    total, sent = call(totals_kernel, [(share, F32), (share, BF16)], queries, *mine)
    totals = [lax.ppermute(sent, "outer", [(z, (z + s) % planes) for z in range(planes)])
              for s in reversed(range(1, planes))] + [total]
    below, whole = call(planes_kernel, [(share, F32)] * 2, *totals)
    groups = [lax.ppermute(whole, "chain", [(c, c ^ d) for c in range(chains)]) for d in range(1, chains)]
    leads = lax.axis_index("chain") == 0
    output = (queries.shape, BF16)

    def way_back(onto, *bases):
        before = call(functools.partial(prefix_kernel, inner), [(share, BF16)] * inner, *mine, *bases,
                      scratch=[pltpu.VMEM((inner,) + share, F32)])
        prefix = swapped(before, "inner", before[0])
        intra = call(intra_kernel, (queries.shape, F32), queries, keys, values,
                     flops=4 * rows * rows * HEADS * HEAD_DIM)
        prefix = call(functools.partial(settle_kernel, inner), ((inner,) + share, BF16), *prefix)
        return call(attend_kernel, output, queries, intra, prefix, result=pltpu.HBM, onto=onto,
                    flops=2 * rows * SLAB * HEADS * HEAD_DIM,
                    scratch=[pltpu.VMEM(*output), pltpu.SemaphoreType.DMA((HEADS * HEAD_DIM // SLAB,))])

    out = lax.cond(leads, lambda: way_back(None, below), lambda: call(unused_kernel, output, result=pltpu.HBM))
    out, groups = lax.optimization_barrier((out, groups))
    return lax.cond(leads, lambda out: out, lambda out: way_back(out, below, *groups), out)


def solution(mesh):
    wide, chains = mesh.devices.shape
    inner = 4
    planes = wide // inner
    finer = jax.sharding.Mesh(mesh.devices.reshape(planes, inner, chains), ("outer", "inner", "chain"))
    spec = P(("chain", "outer", "inner"), None)
    return jax.shard_map(
        functools.partial(per_device, chains, planes, inner),
        mesh=finer,
        in_specs=(spec, spec, spec),
        out_specs=spec,
        check_vma=False,
    )
```
